128 devices in a mesh: row: 8 (over x, core), col: 16 (over y, z).
Axes of the slice: x: 4, y: 4, z: 4, core: 2. Of those that a mesh axis runs over, the one named last changes fastest.
Arguments:
- heights: float32 [2048, 4096], P('row', 'col'), may hold values from -2 to 2
- shadow: int32 [2048, 4096], P('row', 'col'), may hold values 0 or 1
- image_tiles: bfloat16 [8192, 256, 256], P(('row', 'col')), may hold values from 0.019897461 to 0.59765625
- image_dest: int32 [8192, 1], P(('row', 'col')), may hold values from 0 to 127; in each aligned block of 64 rows (0 to 63, 64 to 127, ...) at most 2 rows name the same one
- sun_gain: bfloat16 [8192, 4], P(('row', 'col')), may hold values from -1 to 2.5, as said below
- shot_dest: int32 [32768, 1], P(('row', 'col')), may hold values from 0 to 127; in each aligned block of 256 rows (0 to 255, 256 to 511, ...) at most 4 rows name the same one
- shot_pixel: int32 [32768], P(('row', 'col')), may hold values from 0 to 65535
- shot_height: float32 [32768], P(('row', 'col')), may hold values from -2 to 2
Outputs:
- surface: float32 [2048, 4096], P('row', 'col')
The draws below stay inside these ranges and needn't reach their ends.
Inputs may be any that keep to these rules, and one draw needn't show every extreme that they name: `image_dest`: among one device's 64 image tiles, no tile owner is named more than 2 times. `shot_dest`: among one device's 256 laser shots, no tile owner is named more than 4 times. `sun_gain`: each row is a unit sun direction with elevation between 0.02 and 0.35 radians, followed by a gain between 0.4 and 2.5.
All inputs are finite; a program needn't handle non-finite values. No bound on the sum of `shadow` on one device may be relied on, other than what follows from the above.
Results may differ from the reference program's by a relative error of at most 0.0015.
Values may be sent and summed in bfloat16 or wider, within the bound.
No kernel may reach another device: no remote copies, remote signals or barrier semaphores. Data moves between devices by JAX's collectives and lax.ppermute only.
A program may use at most 256 MiB of HBM per device.

```python
import math
import jax
import jax.numpy as jnp
import numpy as np
from jax import lax

TILE = 256
IMG_DEV = 64
SHOT_DEV = 256
ITERS = 2
CAP = 2
SCAP = 4
IMAGES = 8192
SHOTS = 32768
NH = 2048
NW = 4096
N_ROW = 8
N_COL = 16
DEVICES = 128


def draw_sun_gain(key, part):
    key = jax.random.fold_in(key, 7)
    key_a, key_b, key_c = jax.random.split(key, 3)
    azimuth = jax.random.uniform(key_a, (IMAGES,), jnp.float32, -math.pi, math.pi)
    elevation = jnp.exp(jax.random.uniform(key_b, (IMAGES,), jnp.float32, math.log(0.03), math.log(0.3)))
    gain = jnp.exp(jax.random.uniform(key_c, (IMAGES,), jnp.float32, math.log(0.5), math.log(2.0)))
    flat = jnp.cos(elevation)
    table = jnp.stack([flat * jnp.cos(azimuth), flat * jnp.sin(azimuth), jnp.sin(elevation), gain], axis=1)
    return table.astype(jnp.bfloat16)


def set_ends(array, own_key, smallest, largest):
    spot = [jax.random.randint(jax.random.fold_in(own_key, axis), (), 0, length) for axis, length in enumerate(array.shape)]
    longest = array.shape.index(max(array.shape))
    neighbour = spot[:longest] + [(spot[longest] + 1) % array.shape[longest]] + spot[longest + 1:]
    return array.at[tuple(spot)].set(smallest).at[tuple(neighbour)].set(largest)


def block_scale(key, shape, cuts, low, top_value):
    def one(axis_at, parts):
        steps = jax.random.uniform(jax.random.fold_in(jax.random.fold_in(key, 6), axis_at), (parts,), jnp.float32, low / len(cuts), top_value / len(cuts))
        return jnp.repeat(jnp.exp(steps), shape[axis_at] // parts).reshape((-1,) + (1,) * (len(shape) - axis_at - 1))

    level = one(*cuts[0])
    for cut in cuts[1:]:
        level = level * one(*cut)
    return level


def routed_block(key, own, number, rows, count, top, bound, slope):
    sequence = jax.random.permutation(key, count)
    heavy_load, usual = shares(count, rows * top, bound, slope, True), shares(count, rows * top, bound, slope, False)
    places = jnp.arange(count)

    def named(tallies, rotation):
        used = int((tallies > 0).sum())
        fixed = max(1, used // 4)
        passed = fixed + (places - fixed + rotation * (used - fixed)) % max(1, count - fixed)
        return jnp.zeros((count,), jnp.int32).at[sequence[jnp.where(places < fixed, places, passed)]].set(jnp.asarray(tallies, jnp.int32))

    tallies = jnp.where(number % 4 == 0, named(heavy_load, number // 4), named(usual, number - number // 4 - 1))
    mixed = jax.random.permutation(jax.random.fold_in(own, 3), count)
    giver, receiver = mixed[0:count // 2 * 2:2], mixed[1:count // 2 * 2:2]
    margin = jnp.minimum(tallies[giver] - 1, bound - tallies[receiver]) // 2
    margin = jnp.where((giver == sequence[0]) | (receiver == sequence[0]) | (tallies[receiver] == 0), 0, jnp.maximum(margin, 0))
    passed = jax.random.randint(jax.random.fold_in(own, 4), (count // 2,), 0, 1 << 20) % (margin + 1)
    tallies = tallies.at[giver].add(-passed).at[receiver].add(passed)
    members = jnp.searchsorted(jnp.cumsum(tallies), jnp.arange(rows * top), side="right").astype(jnp.int32)
    table = members.reshape(top, rows).T
    table = table[jax.random.permutation(jax.random.fold_in(own, 1), rows)]
    rotation = jax.random.randint(jax.random.fold_in(own, 2), (rows, 1), 0, top)
    return jnp.take_along_axis(table, (jnp.arange(top)[None, :] + rotation) % top, axis=1)


def shares(amount, total, limit, skew, full):
    loads = [(1 << 20) // math.isqrt(standing ** skew) + 1 for standing in range(1, amount + 1)]
    largest = limit if full else min(limit, max(-(-total // amount), total * loads[0] // sum(loads)))
    least = 1 if total - largest >= amount - 1 else 0
    counts, surplus = [largest] + [least] * (amount - 1), total - largest - least * (amount - 1)
    while surplus > 0:
        movable = [i for i in range(1, amount) if counts[i] < largest] or [i for i in range(1, amount) if counts[i] < limit]
        mass, budget = sum([loads[i] for i in movable]), surplus
        for i in movable:
            extra = min(limit - counts[i], max(1, budget * loads[i] // mass), surplus)
            counts[i] = counts[i] + extra
            surplus = surplus - extra
    return np.array(counts)


def normal_values(own_key, extent, width, reach, cuts=(), dtype=jnp.bfloat16):
    drawn = width * jax.random.normal(own_key, extent, jnp.float32)
    if cuts:
        drawn = drawn * block_scale(own_key, extent, cuts, -0.22, 0.18)
    return jnp.clip(drawn, -reach, reach).astype(dtype)


def setup_inputs(seed: int = 0) -> dict:
    key_of = jax.random.split(jax.random.key(seed), 9)
    heights = normal_values(key_of[0], (NH, NW), 0.3, 2.0, ((0, 8), (1, 16)), jnp.float32)
    shadow = set_ends((jax.random.randint(key_of[1], (NH, NW), 0, 8) < 1).astype(jnp.int32), jax.random.fold_in(key_of[1], 1), 0, 1)
    image_tiles = jnp.clip(0.019897461 + 0.5777588 * jax.random.uniform(key_of[2], (IMAGES, TILE, TILE), jnp.float32) ** block_scale(key_of[2], (IMAGES, TILE, TILE), ((0, 128),), -0.2, 0.2), 0.019897461, 0.59765625).astype(jnp.bfloat16)
    image_dest_keys = jax.random.split(jax.random.fold_in(key_of[3], 1), IMAGES // IMG_DEV)
    image_dest_turns = jax.random.permutation(jax.random.fold_in(key_of[3], 3), IMAGES // IMG_DEV)
    image_dest = jax.vmap(lambda own, number: routed_block(jax.random.fold_in(key_of[3], 2), own, number, IMG_DEV, DEVICES, 1, CAP, 2))(image_dest_keys, image_dest_turns).reshape((IMAGES, 1))
    sun_gain = draw_sun_gain(jax.random.fold_in(key_of[8], 71), 0)
    shot_dest_keys = jax.random.split(jax.random.fold_in(key_of[5], 1), SHOTS // SHOT_DEV)
    shot_dest_turns = jax.random.permutation(jax.random.fold_in(key_of[5], 3), SHOTS // SHOT_DEV)
    shot_dest = jax.vmap(lambda own, number: routed_block(jax.random.fold_in(key_of[5], 2), own, number, SHOT_DEV, DEVICES, 1, SCAP, 1))(shot_dest_keys, shot_dest_turns).reshape((SHOTS, 1))
    shot_pixel = set_ends(jax.random.randint(key_of[6], (SHOTS,), 0, TILE * TILE), jax.random.fold_in(key_of[6], 1), 0, (TILE * TILE) - 1).astype(jnp.int32)
    shot_height = normal_values(key_of[7], (SHOTS,), 0.3, 2.0, ((0, 128),), jnp.float32)
    return dict(heights=heights, shadow=shadow, image_tiles=image_tiles, image_dest=image_dest, sun_gain=sun_gain, shot_dest=shot_dest, shot_pixel=shot_pixel, shot_height=shot_height)


sharpness = 8.0
step_size = 0.01
smooth_weight = 2.0
laser_weight = 20.0

def to_tiles(field):
    return field.reshape(N_ROW, TILE, N_COL, TILE).transpose(0, 2, 1, 3).reshape(N_ROW * N_COL, TILE, TILE)

def from_tiles(stacked):
    return stacked.reshape(N_ROW, N_COL, TILE, TILE).transpose(0, 2, 1, 3).reshape(N_ROW * TILE, N_COL * TILE)

def surface_terms(padded, center):
    slope_x = (padded[1:-1, 2:] - padded[1:-1, :-2]) * 0.5
    slope_y = (padded[2:, 1:-1] - padded[:-2, 1:-1]) * 0.5
    laplace = padded[2:, 1:-1] + padded[:-2, 1:-1] + padded[1:-1, 2:] + padded[1:-1, :-2] - 4.0 * center
    return (slope_x, slope_y, laplace)

def image_terms(slope_x, slope_y, pieces, angles):
    sun_x = angles[:, 0, None, None]
    sun_y = angles[:, 1, None, None]
    sun_z = angles[:, 2, None, None]
    gain = angles[:, 3, None, None]
    inverse = lax.rsqrt(1.0 + slope_x * slope_x + slope_y * slope_y)
    cosine = (sun_z - slope_x * sun_x - slope_y * sun_y) * inverse
    refl = jax.nn.softplus(sharpness * cosine) / sharpness
    sigma = jax.nn.sigmoid(sharpness * cosine)
    along_x = -sun_x * inverse - cosine * slope_x * inverse * inverse
    along_y = -sun_y * inverse - cosine * slope_y * inverse * inverse
    observed = pieces.astype(jnp.float32)
    seen = gain * observed * sigma
    model = gain * gain * refl * sigma
    return (seen * along_x, seen * along_y, model * along_x, model * along_y, gain * observed * refl, gain * gain * refl * refl)

def reference(heights, shadow, image_tiles, image_dest, sun_gain, shot_dest, shot_pixel, shot_height):
    lit = 1.0 - shadow.astype(jnp.float32)
    block = 128 if IMAGES % 128 == 0 else IMAGES
    groups = IMAGES // block
    pixels = image_tiles.reshape(groups, block, TILE, TILE)
    geometry = sun_gain.astype(jnp.float32).reshape(groups, block, 4)
    owners = image_dest[:, 0].astype(jnp.int32).reshape(groups, block)
    shot_owner = shot_dest[:, 0].astype(jnp.int32)
    grid_row = shot_owner // N_COL * TILE + shot_pixel // TILE
    grid_col = shot_owner % N_COL * TILE + shot_pixel % TILE
    flat_index = (grid_row * NW + grid_col).astype(jnp.int32)
    hits = jnp.zeros((NH * NW,), jnp.float32).at[flat_index].add(jnp.ones_like(shot_height)).reshape(NH, NW)
    height_sum = jnp.zeros((NH * NW,), jnp.float32).at[flat_index].add(shot_height).reshape(NH, NW)
    surface = heights
    for sweep in range(ITERS):
        padded = jnp.pad(surface, 1)
        slope_x, slope_y, laplace = surface_terms(padded, surface)
        tiles_x = to_tiles(slope_x)
        tiles_y = to_tiles(slope_y)

        def accumulate(carry, group):
            pieces, angles, owner_ids = group
            terms = image_terms(tiles_x[owner_ids], tiles_y[owner_ids], pieces, angles)
            return (tuple((total.at[owner_ids].add(term) for total, term in zip(carry, terms))), None)
        start = tuple((jnp.zeros((DEVICES, TILE, TILE), jnp.float32) for member in range(6)))
        totals, unused = lax.scan(accumulate, start, (pixels, geometry, owners))
        obs_x, obs_y, fit_x, fit_y, cross, power = [from_tiles(total) for total in totals]
        albedo = jnp.sum(lit * cross) / jnp.sum(lit * power)
        grad_x = lit * (albedo * albedo * fit_x - albedo * obs_x)
        grad_y = lit * (albedo * albedo * fit_y - albedo * obs_y)
        pad_x = jnp.pad(grad_x, 1)
        pad_y = jnp.pad(grad_y, 1)
        data = (pad_x[1:-1, :-2] - pad_x[1:-1, 2:]) * 0.5 + (pad_y[:-2, 1:-1] - pad_y[2:, 1:-1]) * 0.5
        surface = surface - step_size * (data - smooth_weight * laplace + laser_weight * (hits * surface - height_sum))
    return surface
```

```python
import functools

import jax
import jax.numpy as jnp
from jax import lax
from jax.experimental import pallas as pl
from jax.experimental.pallas import tpu as pltpu
from jax.sharding import PartitionSpec as P

ITERS = 2

sharpness = 8.0
step_size = 0.01
smooth_weight = 2.0
laser_weight = 20.0

AXES = ("row", "col")
DEVICES = 128
N_COL = 16
TILE = 256
IMG = 64
SLAB = 512
LANES = 128
PIX_ROWS = IMG * SLAB // LANES
EXTRA = 24
REPLY = 32
SHOT_CAP = 4
F32 = jnp.float32
BF16 = jnp.bfloat16


def exchange(value):
    return lax.all_to_all(value, AXES, split_axis=0, concat_axis=0, tiled=True)


def pieces_of(value, count):
    out = []
    for member in range(count):
        head = lax.reduce_precision(value, 8, 7)
        out.append(head.astype(BF16))
        value = value - head
    return out


def edges(value):
    out = []
    for axis, dim in (("row", 0), ("col", 1)):
        devices, length = (lax.axis_size(axis), value.shape[dim])
        up = [(i, (i + 1) % devices) for i in range(devices - 1)]
        down = [(j, i) for i, j in up]
        last = lax.slice_in_dim(value, length - 1, length, axis=dim)
        first = lax.slice_in_dim(value, 0, 1, axis=dim)
        out.append(lax.ppermute(last, axis, up))
        out.append(lax.ppermute(first, axis, down))
    return out


def laplacian(value, rims):
    above, below, left, right = rims
    tall = jnp.concatenate([above, value, below], axis=0)
    wide = jnp.concatenate([left, value, right], axis=1)
    return tall[2:] + tall[:-2] + wide[:, 2:] + wide[:, :-2] - 4.0 * value


def total_of(terms):
    return (terms[0].astype(F32) + terms[1].astype(F32)) + terms[2].astype(F32)


def own_albedo(cross, power):
    return jnp.where(power > 0.0, cross / jnp.where(power > 0.0, power, 1.0), 0.0)


PACK_ROWS = 16


def pack_kernel(images_ref, extra_ref, out_ref):
    side = 16 * PACK_ROWS
    to = lax.broadcasted_iota(jnp.int32, (side, side), 0)
    source = lax.broadcasted_iota(jnp.int32, (side, side), 1)
    move = jnp.where((to % 16) * 16 + to // 16 == source, 1.0, 0.0).astype(BF16)
    for group in range(IMG // 16):
        block = images_ref[group * 16 : group * 16 + 16].reshape(side, TILE)
        turned = jnp.dot(move, block, preferred_element_type=F32).astype(BF16)
        for r in range(PACK_ROWS):
            for half in range(TILE // LANES):
                quarter = (r % 2) * 2 + half
                place = quarter * IMG + group * 16
                out_ref[r // 2, place : place + 16, :] = turned[
                    r * 16 : r * 16 + 16, half * LANES : half * LANES + LANES
                ]
    out_ref[:, PIX_ROWS : PIX_ROWS + EXTRA, :] = extra_ref[...]


def pack(images, extra):
    per_step = PACK_ROWS * TILE // SLAB
    return pl.pallas_call(
        pack_kernel,
        grid=(DEVICES // per_step,),
        in_specs=[
            pl.BlockSpec((IMG, PACK_ROWS, TILE), lambda s: (0, s, 0)),
            pl.BlockSpec((per_step, EXTRA, LANES), lambda s: (s, 0, 0)),
        ],
        out_specs=pl.BlockSpec((per_step, PIX_ROWS + EXTRA, LANES), lambda s: (s, 0, 0)),
        out_shape=jax.ShapeDtypeStruct((DEVICES, PIX_ROWS + EXTRA, LANES), BF16),
        compiler_params=pltpu.CompilerParams(vmem_limit_bytes=48 * 1024 * 1024),
    )(images, extra)


SUM_SRC = 8
SUM_IMG = SUM_SRC * IMG


def sum_kernel(meta_ref, pixels_ref, normal_ref, sums_ref, plain_ref):
    @pl.when(pl.program_id(0) == 0)
    def start():
        sums_ref[...] = jnp.zeros_like(sums_ref)
        plain_ref[...] = jnp.zeros_like(plain_ref)

    meta = meta_ref[...]
    cols = meta.T
    lane = lax.broadcasted_iota(jnp.int32, (SUM_IMG, DEVICES), 1).astype(F32)
    hot = lane == cols[:, 0:1]
    pick = jnp.concatenate(
        [jnp.where(hot, cols[:, j : j + 1], 0.0).astype(BF16) for j in (1, 2, 3)] * 2, axis=1
    )
    sub = lax.broadcasted_iota(jnp.int32, (DEVICES, SUM_IMG), 0).astype(F32)
    hot_t = sub == meta[0:1, :]
    pick_t = jnp.concatenate(
        [jnp.where(hot_t, meta[j : j + 1, :], 0.0).astype(BF16) for j in (1, 2, 3)], axis=0
    )
    ones_t = jnp.where(hot_t, 1.0, 0.0).astype(BF16)
    gain = cols[:, 4:5]

    half_angle = jnp.dot(pick, normal_ref[...], preferred_element_type=F32)
    bend = jnp.tanh(half_angle)
    rest = 0.5 - 0.5 * bend
    refl = jnp.log(rest) * (gain * (-1.0 / sharpness))
    sigma = (0.5 + 0.5 * bend) * gain
    seen = jnp.concatenate(
        [
            pixels_ref[:, q * IMG : q * IMG + IMG, :].reshape(SUM_IMG, LANES)
            for q in range(SLAB // LANES)
        ],
        axis=1,
    ).astype(F32)
    weighted = jnp.concatenate([(seen * sigma).astype(BF16), (refl * sigma).astype(BF16)], axis=1)
    squares = jnp.concatenate([(seen * refl).astype(BF16), (refl * refl).astype(BF16)], axis=1)
    sums_ref[...] += jnp.dot(pick_t, weighted, preferred_element_type=F32)
    plain_ref[...] += jnp.dot(ones_t, squares, preferred_element_type=F32)


def image_sums(meta, pixels, normals):
    return pl.pallas_call(
        sum_kernel,
        grid=(DEVICES // SUM_SRC,),
        in_specs=[
            pl.BlockSpec((8, SUM_IMG), lambda s: (0, s)),
            pl.BlockSpec((SUM_SRC, PIX_ROWS + EXTRA, LANES), lambda s: (s, 0, 0)),
            pl.BlockSpec((6 * DEVICES, SLAB), lambda s: (0, 0)),
        ],
        out_specs=[
            pl.BlockSpec((3 * DEVICES, 2 * SLAB), lambda s: (0, 0)),
            pl.BlockSpec((DEVICES, 2 * SLAB), lambda s: (0, 0)),
        ],
        out_shape=[
            jax.ShapeDtypeStruct((3 * DEVICES, 2 * SLAB), F32),
            jax.ShapeDtypeStruct((DEVICES, 2 * SLAB), F32),
        ],
        compiler_params=pltpu.CompilerParams(vmem_limit_bytes=56 * 1024 * 1024),
    )(meta, pixels, normals)


def shift_tiles(value, count):
    pad = jnp.zeros((abs(count),) + value.shape[1:], value.dtype)
    if count > 0:
        return jnp.concatenate([pad, value[:-count]], axis=0)
    return jnp.concatenate([value[-count:], pad], axis=0)


def central_x(value):
    column = lax.broadcasted_iota(jnp.int32, (DEVICES, 1), 0) % N_COL
    before = jnp.where(column == 0, 0.0, shift_tiles(value[:, -1:], 1))
    after = jnp.where(column == N_COL - 1, 0.0, shift_tiles(value[:, :1], -1))
    wide = jnp.concatenate([before, value, after], axis=1)
    return wide[:, 2:] - wide[:, :-2]


def slab_slopes(rows, me):
    top = jnp.where(me == 0, shift_tiles(rows[0], N_COL), rows[0])
    bottom = jnp.where(me == DEVICES - 1, shift_tiles(rows[3], -N_COL), rows[3])
    slope_x = jnp.concatenate([central_x(rows[1]), central_x(rows[2])], axis=1) * 0.5
    slope_y = jnp.concatenate([rows[2] - top, bottom - rows[1]], axis=1) * 0.5
    return slope_x, slope_y


def slab_pass(rows, lit, meta, pixels, me):
    slope_x, slope_y = slab_slopes(rows, me)
    inverse = lax.rsqrt(1.0 + slope_x * slope_x + slope_y * slope_y)
    scale = 0.5 * sharpness
    normals = jnp.concatenate(
        [-slope_x * inverse * scale, -slope_y * inverse * scale, inverse * scale], axis=0
    )
    sums, plain = image_sums(meta, pixels, jnp.concatenate(pieces_of(normals, 2), axis=0))
    cross = pieces_of(jnp.sum(lit * plain[:, :SLAB]), 3)
    power = pieces_of(jnp.sum(lit * plain[:, SLAB:]), 3)
    guess = own_albedo(total_of(cross), total_of(power))
    fields = []
    for part in range(2):
        by_x, by_y, by_z = (
            sums[j * DEVICES : (j + 1) * DEVICES, part * SLAB : (part + 1) * SLAB] for j in range(3)
        )
        turned = (by_z - slope_x * by_x - slope_y * by_y) * inverse * inverse * inverse
        grad_x = -lit * (by_x * inverse + slope_x * turned)
        grad_y = -lit * (by_y * inverse + slope_y * turned)
        across = jnp.concatenate([central_x(grad_x[:, :TILE]), central_x(grad_x[:, TILE:])], axis=1)
        halo = jnp.where(
            me == 0, shift_tiles(grad_y[:, :TILE], -N_COL), shift_tiles(grad_y[:, TILE:], N_COL)
        )
        fields.append(jnp.concatenate([across * (-0.5), grad_y, halo], axis=1))
    seen, model = fields
    scalars = jnp.broadcast_to(jnp.stack(cross + power)[None, :], (DEVICES, 6))
    flat = jnp.concatenate(
        [model.astype(BF16)]
        + pieces_of(guess * model - seen, 2)
        + [scalars, jnp.zeros((DEVICES, 2 * LANES - 6), BF16)],
        axis=1,
    )
    return flat.reshape(DEVICES, REPLY, LANES)


def owner_data(got):
    flat = got.reshape(DEVICES, REPLY * LANES).astype(F32)
    width = 2 * SLAB + TILE
    terms = flat[:, 3 * width : 3 * width + 6]
    cross = terms[:, 0:1] + terms[:, 1:2] + terms[:, 2:3]
    power = terms[:, 3:4] + terms[:, 4:5] + terms[:, 5:6]
    guess = own_albedo(cross, power)
    albedo = jnp.sum(cross) / jnp.sum(power)
    model = flat[:, :width]
    misfit = flat[:, width : 2 * width] + flat[:, 2 * width : 3 * width]
    grad = albedo * misfit + albedo * (albedo - guess) * model
    across = grad[:, :SLAB].reshape(TILE, TILE)
    along = grad[:, SLAB : 2 * SLAB].reshape(TILE, TILE)
    halo = grad[:, 2 * SLAB :]
    tall = jnp.concatenate([halo[-1:], along, halo[:1]], axis=0)
    return across + (tall[:-2] - tall[2:]) * 0.5


def slab_rows(surface):
    tall = jnp.concatenate([surface[-1:], surface, surface[:1]], axis=0)
    four = jnp.stack([tall[j : j + TILE : 2] for j in range(4)], axis=1).reshape(DEVICES, 8, LANES)
    return jnp.concatenate(pieces_of(four, 2), axis=1)


def shot_sums(slots):
    cell = lax.broadcasted_iota(jnp.int32, (1, TILE), 1).astype(F32)
    present = slots[:, 4:5]
    in_row = jnp.where(slots[:, 0:1] == cell, 1.0, 0.0)
    in_col = jnp.where(slots[:, 1:2] == cell, 1.0, 0.0).astype(BF16)
    left = jnp.concatenate([in_row * slots[:, j : j + 1] * present for j in (4, 2, 3)], axis=1)
    both = lax.dot_general(
        left.astype(BF16), in_col, (((0,), (0,)), ((), ())), preferred_element_type=F32
    )
    return both[:TILE], both[TILE : 2 * TILE] + both[2 * TILE :]


def shot_slots(shot_dest, shot_pixel, shot_height):
    count = shot_dest.shape[0]
    target = shot_dest[:, 0]
    before = jnp.arange(count)[None, :] < jnp.arange(count)[:, None]
    alike = target[None, :] == target[:, None]
    rank = jnp.sum(jnp.logical_and(before, alike), axis=1)
    place = target * SHOT_CAP + rank
    slots = jnp.arange(DEVICES * SHOT_CAP)[:, None] == place[None, :]
    high, low = pieces_of(shot_height, 2)
    record = jnp.stack(
        [
            (shot_pixel // TILE).astype(BF16),
            (shot_pixel % TILE).astype(BF16),
            high,
            low,
            jnp.ones_like(high),
        ],
        axis=1,
    )
    got = jnp.dot(slots.astype(BF16), record, preferred_element_type=F32).astype(BF16)
    return got.reshape(DEVICES, SHOT_CAP * 5)


def body(heights, shadow, image_tiles, image_dest, sun_gain, shot_dest, shot_pixel, shot_height):
    me = lax.axis_index("row") * N_COL + lax.axis_index("col")
    lit = 1.0 - shadow.astype(F32)
    rims = edges(heights)

    def fan(value):
        return jnp.broadcast_to(value[None], (DEVICES,) + value.shape)

    dest = image_dest[:, 0].astype(BF16)
    shots = shot_slots(shot_dest, shot_pixel, shot_height)
    extra = jnp.concatenate(
        [
            slab_rows(heights),
            lit.astype(BF16).reshape(DEVICES, 4, LANES),
            fan(jnp.concatenate([dest, jnp.zeros_like(dest)])[None]),
            fan(sun_gain.T.reshape(2, LANES)),
            jnp.pad(shots, ((0, 0), (0, LANES - shots.shape[1])))[:, None, :],
        ],
        axis=1,
    )
    pixels = exchange(pack(image_tiles, extra))
    extra = pixels[:, PIX_ROWS:, :]
    meta = jnp.stack(
        [
            extra[:, 20, :IMG],
            extra[:, 21, :IMG],
            extra[:, 21, IMG:],
            extra[:, 22, :IMG],
            extra[:, 22, IMG:],
        ]
    ).astype(F32)
    meta = jnp.pad(meta.reshape(5, DEVICES * IMG), ((0, 3), (0, 0)))
    slab_lit = extra[:, 16:20, :].reshape(DEVICES, SLAB).astype(F32)
    around = extra[:, 0:16, :]
    slots = extra[:, 23, : SHOT_CAP * 5].reshape(DEVICES * SHOT_CAP, 5).astype(F32)
    hits, height_sum = shot_sums(slots)
    surface = heights
    for sweep in range(ITERS):
        if sweep > 0:
            around = exchange(slab_rows(surface))
            rims = edges(surface)
        fine = (around[:, :8].astype(F32) + around[:, 8:].astype(F32)).reshape(DEVICES, 4, TILE)
        rows = [fine[:, j] for j in range(4)]
        got = exchange(slab_pass(rows, slab_lit, meta, pixels, me))
        data = owner_data(got)
        laplace = laplacian(surface, rims)
        surface = surface - step_size * (
            data - smooth_weight * laplace + laser_weight * (hits * surface - height_sum)
        )
    return surface


def solution(mesh):
    placed = (
        P("row", "col"),
        P("row", "col"),
        P(("row", "col"), None, None),
        P(("row", "col"), None),
        P(("row", "col"), None),
        P(("row", "col"), None),
        P(("row", "col")),
        P(("row", "col")),
    )
    return jax.shard_map(
        body, mesh=mesh, in_specs=placed, out_specs=P("row", "col"), check_vma=False
    )
```

```python
import functools

import jax
import jax.numpy as jnp
from jax import lax
from jax.experimental import pallas as pl
from jax.experimental.pallas import tpu as pltpu
from jax.sharding import PartitionSpec as P

sharpness = 8.0
step_size = 0.01
smooth_weight = 2.0
laser_weight = 20.0

AXES = ("row", "col")
DEVICES = 128
N_COL = 16
TILE = 256
IMG = 64
SLAB = 512
LANES = 128
PIX_ROWS = IMG * SLAB // LANES
EXTRA = 24
REPLY = 32
SHOT_CAP = 4
LOG_2 = 0.6931471805599453
F32 = jnp.float32
BF16 = jnp.bfloat16


def exchange(value):
    return lax.all_to_all(value, AXES, split_axis=0, concat_axis=0, tiled=True)


def edges(value):
    out = []
    for axis, dim in (("row", 0), ("col", 1)):
        devices, length = (lax.axis_size(axis), value.shape[dim])
        up = [(i, (i + 1) % devices) for i in range(devices - 1)]
        down = [(j, i) for i, j in up]
        last = lax.slice_in_dim(value, length - 1, length, axis=dim)
        first = lax.slice_in_dim(value, 0, 1, axis=dim)
        out.append(lax.ppermute(last, axis, up))
        out.append(lax.ppermute(first, axis, down))
    return out


def own_albedo(cross, power):
    return jnp.where(power > 0.0, cross / jnp.where(power > 0.0, power, 1.0), 0.0)


PACK_ROWS = 64


def swap_matrix():
    to = lax.broadcasted_iota(jnp.int32, (256, 256), 0)
    source = lax.broadcasted_iota(jnp.int32, (256, 256), 1)
    return jnp.where((to % 16) * 16 + to // 16 == source, 1.0, 0.0).astype(BF16)


def iota_of(shape, dim):
    return lax.broadcasted_iota(jnp.int32, shape, dim)


def two_terms(value):
    head = value.astype(BF16)
    return head, (value - head.astype(F32)).astype(BF16)


def swapped(swap, pieces):
    turned = jnp.dot(swap, jnp.concatenate(pieces, axis=0), preferred_element_type=F32)
    return turned.astype(BF16).reshape(16, 16, LANES)


def around_pieces(even, odd):
    four = (pltpu.roll(odd, 1, 0), even, odd, pltpu.roll(even, DEVICES - 1, 0))
    terms = [two_terms(item) for item in four]
    return [
        terms[r][term][:, half * LANES : half * LANES + LANES]
        for term in range(2)
        for r in range(4)
        for half in range(2)
    ]


def shot_rows(shots):
    count = shots.shape[1]
    target, pixel, height = shots[0:1], shots[1:2], shots[2:3]
    head = height.astype(BF16).astype(F32)
    grid_row = jnp.floor(pixel * (1.0 / TILE))
    pair = jnp.floor(grid_row * 0.5)
    columns = jnp.concatenate(
        [
            target,
            (grid_row - 2.0 * pair) * DEVICES + pair,
            pixel - TILE * grid_row,
            head,
            height - head,
            jnp.ones_like(height),
            jnp.zeros((2, count), F32),
        ],
        axis=0,
    ).T
    alike = columns[:, 0:1] == target
    before = iota_of((count, count), 0) < iota_of((count, count), 1)
    rank = jnp.sum(jnp.where(jnp.logical_and(alike, before), 1.0, 0.0), axis=0, keepdims=True)
    lane = iota_of((count, LANES), 1)
    record = jnp.zeros((count, LANES), F32)
    for member in range(5):
        record = jnp.where(lane % 5 == member, columns[:, member + 1 : member + 2], record)
    owned = iota_of((DEVICES, count), 0).astype(F32) == target
    rows = jnp.zeros((DEVICES, LANES), F32)
    for slot in range(SHOT_CAP):
        chosen = jnp.where(jnp.logical_and(owned, rank == slot), 1.0, 0.0).astype(BF16)
        held = jnp.where(lane // 5 == slot, record, 0.0).astype(BF16)
        rows = rows + jnp.dot(chosen, held, preferred_element_type=F32)
    return rows.astype(BF16)


def pack_kernel(images_ref, heights_ref, shadow_ref, table_ref, shots_ref, out_ref, split_ref, extra_ref, halves_ref):
    step = pl.program_id(0)
    swap = swap_matrix()

    @pl.when(step == 0)
    def start():
        tiles = []
        for source, kind in ((heights_ref, 0), (shadow_ref, 1)):
            parts = []
            for half in range(2):
                lanes = slice(half * LANES, half * LANES + LANES)
                block = source[:, lanes]
                halves_ref[kind * 2 + half] = block if kind == 0 else 1.0 - block.astype(F32)
            for side in range(2):
                parts.append(
                    jnp.concatenate(
                        [halves_ref[kind * 2 + half, pl.ds(side, DEVICES, 2), :] for half in range(2)],
                        axis=1,
                    )
                )
            tiles.append(parts)
        (even, odd), (lit_even, lit_odd) = tiles
        split_ref[:DEVICES] = even
        split_ref[DEVICES:] = odd
        first = around_pieces(even, odd)
        lit = jnp.concatenate([lit_even, lit_odd], axis=1).astype(BF16)
        table = table_ref[...].astype(BF16)
        second = [lit[:, j * LANES : j * LANES + LANES] for j in range(4)]
        second += [jnp.broadcast_to(table[j : j + 1], (DEVICES, LANES)) for j in range(3)]
        second += [shot_rows(shots_ref[...])] + [jnp.zeros((DEVICES, LANES), BF16)] * 8
        for group in range(DEVICES // 16):
            span = slice(group * 16, group * 16 + 16)
            extra_ref[span, 0:16] = swapped(swap, [item[span] for item in first])
            extra_ref[span, 16:32] = swapped(swap, [item[span] for item in second])

    for band in range(PACK_ROWS // 16):
        for group in range(IMG // 16):
            block = images_ref[group * 16 : group * 16 + 16, band * 16 : band * 16 + 16]
            turned = jnp.dot(
                swap, block.reshape(256, TILE), preferred_element_type=F32
            ).astype(BF16)
            for r in range(16):
                for half in range(TILE // LANES):
                    place = ((r % 2) * 2 + half) * IMG + group * 16
                    out_ref[band * 8 + r // 2, place : place + 16, :] = turned[
                        r * 16 : r * 16 + 16, half * LANES : half * LANES + LANES
                    ]
    per_step = PACK_ROWS // 2
    here = pl.ds(pl.multiple_of(step * per_step, per_step), per_step)
    out_ref[:, PIX_ROWS : PIX_ROWS + EXTRA, :] = extra_ref[here, 0:EXTRA, :]


def pack(images, heights, shadow, table, shots):
    per_step = PACK_ROWS // 2
    whole = lambda s: (0, 0)
    return pl.pallas_call(
        pack_kernel,
        grid=(DEVICES // per_step,),
        in_specs=[
            pl.BlockSpec((IMG, PACK_ROWS, TILE), lambda s: (0, s, 0)),
            pl.BlockSpec((TILE, TILE), whole),
            pl.BlockSpec((TILE, TILE), whole),
            pl.BlockSpec((8, LANES), whole),
            pl.BlockSpec((8, TILE), whole),
        ],
        out_specs=[
            pl.BlockSpec((per_step, PIX_ROWS + EXTRA, LANES), lambda s: (s, 0, 0)),
            pl.BlockSpec((TILE, TILE), whole),
        ],
        out_shape=[
            jax.ShapeDtypeStruct((DEVICES, PIX_ROWS + EXTRA, LANES), BF16),
            jax.ShapeDtypeStruct((TILE, TILE), F32),
        ],
        scratch_shapes=[
            pltpu.VMEM((DEVICES, 32, LANES), BF16),
            pltpu.VMEM((4, TILE, LANES), F32),
        ],
        compiler_params=pltpu.CompilerParams(vmem_limit_bytes=48 * 1024 * 1024),
    )(images, heights, shadow, table, shots)


SUM_SRC = 16
SUM_IMG = SUM_SRC * IMG
HALF_SRC = SUM_SRC // 2
HALF_IMG = SUM_IMG // 2
CHUNKS = 4
WIDTH = 2 * SLAB + TILE


def sideways(value):
    lane = iota_of(value.shape, 1)
    column = iota_of(value.shape, 0) % N_COL
    before = pltpu.roll(value, 1, 1)
    first = jnp.where(column == 0, 0.0, pltpu.roll(before, 1, 0))
    after = pltpu.roll(value, TILE - 1, 1)
    last = jnp.where(column == N_COL - 1, 0.0, pltpu.roll(after, DEVICES - 1, 0))
    return jnp.where(lane == 0, first, before), jnp.where(lane == TILE - 1, last, after)


def central_x(value):
    before, after = sideways(value)
    return after - before


def shift_tiles(value, count):
    pad = jnp.zeros((abs(count),) + value.shape[1:], value.dtype)
    if count > 0:
        return jnp.concatenate([pad, value[:-count]], axis=0)
    return jnp.concatenate([value[-count:], pad], axis=0)


def slab_normals(me, around_ref, lit_ref, normal_ref, slopes_ref, rows_ref):
    swap = swap_matrix()
    for group in range(DEVICES // 16):
        span = slice(group * 16, group * 16 + 16)
        turned = jnp.dot(
            swap, around_ref[span].reshape(256, LANES), preferred_element_type=F32
        )
        fine = turned[:128] + turned[128:]
        for r in range(4):
            for half in range(2):
                at = (2 * r + half) * 16
                rows_ref[r, span, half * LANES : half * LANES + LANES] = fine[at : at + 16]
    rows = [rows_ref[r] for r in range(4)]
    top = jnp.where(me == 0, shift_tiles(rows[0], N_COL), rows[0])
    bottom = jnp.where(me == DEVICES - 1, shift_tiles(rows[3], -N_COL), rows[3])
    slope_x = jnp.concatenate([central_x(rows[1]), central_x(rows[2])], axis=1) * 0.5
    slope_y = jnp.concatenate([rows[2] - top, bottom - rows[1]], axis=1) * 0.5
    inverse = lax.rsqrt(1.0 + slope_x * slope_x + slope_y * slope_y)
    slopes_ref[0], slopes_ref[1], slopes_ref[2] = slope_x, slope_y, inverse
    scale = 0.5 * sharpness
    x_head, x_tail = two_terms(-slope_x * inverse * scale)
    y_head, y_tail = two_terms(-slope_y * inverse * scale)
    steep = ((inverse - 1.0) * scale).astype(BF16)
    flat = jnp.where(lit_ref[...] > 0.5, scale, -2048.0).astype(BF16)
    for place, item in enumerate((x_head, y_head, x_tail, y_tail, steep, flat)):
        normal_ref[place * DEVICES : (place + 1) * DEVICES] = item


def slab_reply(me, lit_ref, slopes_ref, sums_ref, plain_ref, reply_ref):
    lit = lit_ref[...]
    slope_x, slope_y, inverse = slopes_ref[0], slopes_ref[1], slopes_ref[2]
    cube = inverse * inverse * inverse
    lane = iota_of((16, LANES), 1)
    scalars = jnp.zeros((16, LANES), BF16)
    totals = []
    for part in range(2):
        value = jnp.sum(plain_ref[:, part * SLAB : (part + 1) * SLAB], keepdims=True)
        total = jnp.zeros((1, 1), F32)
        for term in range(3):
            head = value.astype(BF16).astype(F32)
            scalars = jnp.where(lane == part * 3 + term, head, scalars.astype(F32)).astype(BF16)
            value = value - head
            total = total + head
        totals.append(total)
    guess = own_albedo(totals[0], totals[1])
    fields = []
    for part in range(2):
        by_x, by_y, by_z = (
            sums_ref[j * DEVICES : (j + 1) * DEVICES, part * SLAB : (part + 1) * SLAB]
            for j in range(3)
        )
        turned = (by_z - slope_x * by_x - slope_y * by_y) * cube
        grad_x = -lit * (by_x * inverse + slope_x * turned)
        grad_y = -lit * (by_y * inverse + slope_y * turned)
        across = jnp.concatenate([central_x(grad_x[:, :TILE]), central_x(grad_x[:, TILE:])], axis=1)
        halo = jnp.where(
            me == 0, shift_tiles(grad_y[:, :TILE], -N_COL), shift_tiles(grad_y[:, TILE:], N_COL)
        )
        fields.append(jnp.concatenate([across * (-0.5), grad_y, halo], axis=1))
    seen, model = fields
    head, tail = two_terms(guess * model - seen)
    flat = jnp.concatenate([model.astype(BF16), head, tail], axis=1)
    swap = swap_matrix()
    for group in range(DEVICES // 16):
        span = slice(group * 16, group * 16 + 16)
        pieces = [flat[span, j * LANES : (j + 1) * LANES] for j in range(30)]
        pieces = pieces + [scalars, jnp.zeros((16, LANES), BF16)]
        for part in range(2):
            block = jnp.concatenate(pieces[part * 16 : part * 16 + 16], axis=0)
            turned = jnp.dot(swap, block, preferred_element_type=F32).astype(BF16)
            reply_ref[span, part * 16 : part * 16 + 16, :] = turned.reshape(16, 16, LANES)


def sum_kernel(
    me_ref, meta_ref, pixels_ref, around_ref, lit_ref, reply_ref,
    normal_ref, slopes_ref, rows_ref, sums_ref, plain_ref, first_w, second_w, first_p, second_p,
):
    step = pl.program_id(0)
    me = me_ref[0]

    @pl.when(step == 0)
    def start():
        sums_ref[...] = jnp.zeros_like(sums_ref)
        plain_ref[...] = jnp.zeros_like(plain_ref)
        second_w[...] = jnp.zeros_like(second_w)
        second_p[...] = jnp.zeros_like(second_p)
        slab_normals(me, around_ref, lit_ref, normal_ref, slopes_ref, rows_ref)

    def front(side, w_ref, p_ref):
        meta = meta_ref[:, side * HALF_IMG : (side + 1) * HALF_IMG]
        cols = meta.T
        hot = iota_of((HALF_IMG, DEVICES), 1).astype(F32) == cols[:, 0:1]
        sun = [jnp.where(hot, cols[:, j : j + 1], 0.0).astype(BF16) for j in (1, 2, 3)]
        pick = jnp.concatenate([sun[0], sun[1], sun[0], sun[1], sun[2], sun[2]], axis=1)
        hot_t = iota_of((DEVICES, HALF_IMG), 0).astype(F32) == meta[0:1, :]
        for j in range(3):
            p_ref[j * DEVICES : (j + 1) * DEVICES] = jnp.where(
                hot_t, meta[j + 1 : j + 2, :], 0.0
            ).astype(BF16)
        count, images = (HALF_SRC // CHUNKS, HALF_IMG // CHUNKS)
        for chunk in range(CHUNKS):
            span = slice(chunk * images, (chunk + 1) * images)
            src = slice(side * HALF_SRC + chunk * count, side * HALF_SRC + (chunk + 1) * count)
            half_angle = jnp.dot(pick[span], normal_ref[...], preferred_element_type=F32)
            gain = cols[span, 4:5]
            bend = jnp.tanh(half_angle)
            refl = (jnp.log(1.0 - bend) - LOG_2) * (gain * (-1.0 / sharpness))
            sigma = bend * (gain * 0.5) + gain * 0.5
            seen = jnp.concatenate(
                [
                    pixels_ref[src, q * IMG : q * IMG + IMG, :].reshape(images, LANES)
                    for q in range(SLAB // LANES)
                ],
                axis=1,
            ).astype(F32)
            w_ref[span, :SLAB] = (seen * sigma).astype(BF16)
            w_ref[span, SLAB:] = (refl * sigma).astype(BF16)
            plain_ref[:, :SLAB] += jnp.sum((seen * refl).reshape(-1, 8, SLAB), axis=0)
            plain_ref[:, SLAB:] += jnp.sum((refl * refl).reshape(-1, 8, SLAB), axis=0)

    def back(w_ref, p_ref):
        sums_ref[...] += jnp.dot(p_ref[...], w_ref[...], preferred_element_type=F32)

    back(second_w, second_p)
    front(0, first_w, first_p)
    back(first_w, first_p)
    front(1, second_w, second_p)

    @pl.when(step == pl.num_programs(0) - 1)
    def finish():
        back(second_w, second_p)
        slab_reply(me, lit_ref, slopes_ref, sums_ref, plain_ref, reply_ref)


def slab_pass(me, meta, pixels, around, lit):
    return pl.pallas_call(
        sum_kernel,
        grid=(DEVICES // SUM_SRC,),
        in_specs=[
            pl.BlockSpec(memory_space=pltpu.SMEM),
            pl.BlockSpec((8, SUM_IMG), lambda s: (0, s)),
            pl.BlockSpec((SUM_SRC, PIX_ROWS + EXTRA, LANES), lambda s: (s, 0, 0)),
            pl.BlockSpec((DEVICES, 16, LANES), lambda s: (0, 0, 0)),
            pl.BlockSpec((DEVICES, SLAB), lambda s: (0, 0)),
        ],
        out_specs=pl.BlockSpec((DEVICES, REPLY, LANES), lambda s: (0, 0, 0)),
        out_shape=jax.ShapeDtypeStruct((DEVICES, REPLY, LANES), BF16),
        scratch_shapes=[
            pltpu.VMEM((6 * DEVICES, SLAB), BF16),
            pltpu.VMEM((3, DEVICES, SLAB), F32),
            pltpu.VMEM((4, DEVICES, TILE), F32),
            pltpu.VMEM((3 * DEVICES, 2 * SLAB), F32),
            pltpu.VMEM((8, 2 * SLAB), F32),
            pltpu.VMEM((HALF_IMG, 2 * SLAB), BF16),
            pltpu.VMEM((HALF_IMG, 2 * SLAB), BF16),
            pltpu.VMEM((3 * DEVICES, HALF_IMG), BF16),
            pltpu.VMEM((3 * DEVICES, HALF_IMG), BF16),
        ],
        compiler_params=pltpu.CompilerParams(vmem_limit_bytes=48 * 1024 * 1024),
    )(me, meta, pixels, around, lit)


def owner_kernel(final, *refs):
    got_ref, surface_ref, hits_ref, height_ref, ends_ref, sides_ref = refs[:6]
    outs, (model_ref, misfit_ref, scalar_ref, mixed_ref) = refs[6:-4], refs[-4:]
    swap = swap_matrix()
    for group in range(DEVICES // 16):
        span = slice(group * 16, group * 16 + 16)
        rows = []
        for part in range(2):
            block = got_ref[span, part * 16 : part * 16 + 16, :].reshape(256, LANES)
            turned = jnp.dot(swap, block, preferred_element_type=F32)
            rows += [turned[j * 16 : j * 16 + 16] for j in range(16)]
        for j in range(10):
            model_ref[j, span] = rows[j]
            misfit_ref[j, span] = rows[10 + j] + rows[20 + j]
        scalar_ref[span] = rows[30]
    scalars = scalar_ref[...]
    cross = scalars[:, 0:1] + scalars[:, 1:2] + scalars[:, 2:3]
    power = scalars[:, 3:4] + scalars[:, 4:5] + scalars[:, 5:6]
    albedo = jnp.sum(cross, keepdims=True) / jnp.sum(power, keepdims=True)
    rest = albedo * (albedo - own_albedo(cross, power))

    def grad(j):
        return jnp.concatenate(
            [albedo * misfit_ref[i] + rest * model_ref[i] for i in (j, j + 1)], axis=1
        )

    row = iota_of((DEVICES, TILE), 0)
    lane = iota_of((DEVICES, TILE), 1)
    along_even, along_odd, halo = grad(4), grad(6), grad(8)
    before = jnp.where(row == 0, pltpu.roll(halo, 1, 0), pltpu.roll(along_odd, 1, 0))
    after = jnp.where(
        row == DEVICES - 1,
        pltpu.roll(halo, DEVICES - 1, 0),
        pltpu.roll(along_even, DEVICES - 1, 0),
    )
    data = (grad(0) + (before - along_odd) * 0.5, grad(2) + (along_even - after) * 0.5)
    old = (surface_ref[:DEVICES], surface_ref[DEVICES:])
    above = jnp.where(row == 0, ends_ref[0:1], pltpu.roll(old[1], 1, 0))
    below = jnp.where(row == DEVICES - 1, ends_ref[1:2], pltpu.roll(old[0], DEVICES - 1, 0))
    vertical = (above + old[1], old[0] + below)
    new = []
    for part in range(2):
        span = slice(part * DEVICES, (part + 1) * DEVICES)
        left = jnp.where(lane == 0, sides_ref[span, 0:1], pltpu.roll(old[part], 1, 1))
        right = jnp.where(
            lane == TILE - 1, sides_ref[span, 1:2], pltpu.roll(old[part], TILE - 1, 1)
        )
        laplace = vertical[part] + left + right - 4.0 * old[part]
        laser = hits_ref[span] * old[part] - height_ref[span]
        new.append(
            old[part]
            - step_size * (data[part] - smooth_weight * laplace + laser_weight * laser)
        )
    if final:
        for part in range(2):
            for half in range(2):
                lanes = slice(half * LANES, half * LANES + LANES)
                mixed_ref[pl.ds(half * TILE + part, DEVICES, 2), :] = new[part][:, lanes]
        for half in range(2):
            outs[0][:, half * LANES : half * LANES + LANES] = mixed_ref[
                half * TILE : half * TILE + TILE
            ]
        return
    outs[0][:DEVICES], outs[0][DEVICES:] = new[0], new[1]
    pieces = around_pieces(new[0], new[1])
    for group in range(DEVICES // 16):
        span = slice(group * 16, group * 16 + 16)
        outs[1][span] = swapped(swap, [item[span] for item in pieces])


def owner_update(final, got, surface, hits, height_sum, rims):
    above, below, left, right = rims
    ends = jnp.concatenate([above, below], axis=0)
    sides = jnp.concatenate([left, right], axis=1)
    out_shape = [jax.ShapeDtypeStruct((TILE, TILE), F32)]
    if not final:
        out_shape.append(jax.ShapeDtypeStruct((DEVICES, 16, LANES), BF16))
    return pl.pallas_call(
        functools.partial(owner_kernel, final),
        out_shape=out_shape,
        scratch_shapes=[
            pltpu.VMEM((10, DEVICES, LANES), F32),
            pltpu.VMEM((10, DEVICES, LANES), F32),
            pltpu.VMEM((DEVICES, LANES), F32),
            pltpu.VMEM((2 * TILE, LANES), F32),
        ],
        compiler_params=pltpu.CompilerParams(vmem_limit_bytes=32 * 1024 * 1024),
    )(got, surface, hits, height_sum, ends, sides)


def shot_sums(slots):
    cell = lax.broadcasted_iota(jnp.int32, (1, TILE), 1).astype(F32)
    present = slots[:, 4:5]
    in_row = jnp.where(slots[:, 0:1] == cell, 1.0, 0.0)
    in_col = jnp.where(slots[:, 1:2] == cell, 1.0, 0.0).astype(BF16)
    left = jnp.concatenate([in_row * slots[:, j : j + 1] * present for j in (4, 2, 3)], axis=1)
    both = lax.dot_general(
        left.astype(BF16), in_col, (((0,), (0,)), ((), ())), preferred_element_type=F32
    )
    return both[:TILE], both[TILE : 2 * TILE] + both[2 * TILE :]


def body(heights, shadow, image_tiles, image_dest, sun_gain, shot_dest, shot_pixel, shot_height):
    me = (lax.axis_index("row") * N_COL + lax.axis_index("col")).astype(jnp.int32)[None]
    dest = image_dest[:, 0].astype(F32)
    table = jnp.concatenate([dest, jnp.zeros_like(dest), sun_gain.astype(F32).T.reshape(-1)])
    table = jnp.pad(table.reshape(3, LANES), ((0, 5), (0, 0)))
    shots = jnp.stack([shot_dest[:, 0].astype(F32), shot_pixel.astype(F32), shot_height])
    shots = jnp.pad(shots, ((0, 5), (0, 0)))
    packed, surface = pack(image_tiles, heights, shadow, table, shots)
    rims = edges(surface)
    pixels = exchange(packed)
    extra = pixels[:, PIX_ROWS:, :]
    meta = jnp.stack(
        [
            extra[:, 20, :IMG],
            extra[:, 21, :IMG],
            extra[:, 21, IMG:],
            extra[:, 22, :IMG],
            extra[:, 22, IMG:],
        ]
    ).astype(F32)
    meta = jnp.pad(meta.reshape(5, DEVICES * IMG), ((0, 3), (0, 0)))
    slab_lit = extra[:, 16:20, :].reshape(DEVICES, SLAB).astype(F32)
    around = extra[:, 0:16, :]
    slots = extra[:, 23, : SHOT_CAP * 5].reshape(DEVICES * SHOT_CAP, 5).astype(F32)
    hits, height_sum = shot_sums(slots)
    reply = slab_pass(me, meta, pixels, around, slab_lit)
    got = exchange(reply)
    surface, around = owner_update(False, got, surface, hits, height_sum, rims)
    around = exchange(around)
    rims = edges(surface)
    got = exchange(slab_pass(me, meta, pixels, around, slab_lit))
    return owner_update(True, got, surface, hits, height_sum, rims)[0]


def solution(mesh):
    placed = (
        P("row", "col"),
        P("row", "col"),
        P(("row", "col"), None, None),
        P(("row", "col"), None),
        P(("row", "col"), None),
        P(("row", "col"), None),
        P(("row", "col")),
        P(("row", "col")),
    )
    return jax.shard_map(
        body, mesh=mesh, in_specs=placed, out_specs=P("row", "col"), check_vma=False
    )
```

```python
import functools

import jax
import jax.numpy as jnp
from jax import lax
from jax.experimental import pallas as pl
from jax.experimental.pallas import tpu as pltpu
from jax.sharding import PartitionSpec as P

sharpness = 8.0
step_size = 0.01
smooth_weight = 2.0
laser_weight = 20.0

AXES = ("row", "col")
DEVICES = 128
N_COL = 16
TILE = 256
IMG = 64
SLAB = 512
LANES = 128
QUARTERS = SLAB // LANES
PARTS = ((0, 48), (48, 16))
EXTRA = 24
REPLY = 24
SHOT_CAP = 4
LOG_2 = 0.6931471805599453
F32 = jnp.float32
BF16 = jnp.bfloat16


def exchange(value):
    return lax.all_to_all(value, AXES, split_axis=0, concat_axis=0, tiled=True)


def edges(value):
    out = []
    for axis, dim in (("row", 0), ("col", 1)):
        devices, length = (lax.axis_size(axis), value.shape[dim])
        up = [(i, (i + 1) % devices) for i in range(devices - 1)]
        down = [(j, i) for i, j in up]
        last = lax.slice_in_dim(value, length - 1, length, axis=dim)
        first = lax.slice_in_dim(value, 0, 1, axis=dim)
        out.append(lax.ppermute(last, axis, up))
        out.append(lax.ppermute(first, axis, down))
    return out


def own_albedo(cross, power):
    return jnp.where(power > 0.0, cross / jnp.where(power > 0.0, power, 1.0), 0.0)


PACK_ROWS = 64


def swap_matrix(blocks=16, rows=16):
    to = lax.broadcasted_iota(jnp.int32, (blocks * rows, blocks * rows), 0)
    source = lax.broadcasted_iota(jnp.int32, (blocks * rows, blocks * rows), 1)
    return jnp.where((to % blocks) * rows + to // blocks == source, 1.0, 0.0).astype(BF16)


def iota_of(shape, dim):
    return lax.broadcasted_iota(jnp.int32, shape, dim)


def two_terms(value):
    head = value.astype(BF16)
    return head, (value - head.astype(F32)).astype(BF16)


def swapped(swap, pieces):
    turned = jnp.dot(swap, jnp.concatenate(pieces, axis=0), preferred_element_type=F32)
    return turned.astype(BF16).reshape(16, len(pieces), LANES)


def around_pieces(even, odd):
    four = (pltpu.roll(odd, 1, 0), even, odd, pltpu.roll(even, DEVICES - 1, 0))
    terms = [two_terms(item) for item in four]
    return [
        terms[r][term][:, half * LANES : half * LANES + LANES]
        for term in range(2)
        for r in range(4)
        for half in range(2)
    ]


def shot_rows(shots):
    count = shots.shape[1]
    target, pixel, height = shots[0:1], shots[1:2], shots[2:3]
    head = height.astype(BF16).astype(F32)
    grid_row = jnp.floor(pixel * (1.0 / TILE))
    pair = jnp.floor(grid_row * 0.5)
    columns = jnp.concatenate(
        [
            target,
            (grid_row - 2.0 * pair) * DEVICES + pair,
            pixel - TILE * grid_row,
            head,
            height - head,
            jnp.ones_like(height),
            jnp.zeros((2, count), F32),
        ],
        axis=0,
    ).T
    alike = columns[:, 0:1] == target
    before = iota_of((count, count), 0) < iota_of((count, count), 1)
    rank = jnp.sum(jnp.where(jnp.logical_and(alike, before), 1.0, 0.0), axis=0, keepdims=True)
    lane = iota_of((count, LANES), 1)
    record = jnp.zeros((count, LANES), F32)
    for member in range(5):
        record = jnp.where(lane % 5 == member, columns[:, member + 1 : member + 2], record)
    owned = iota_of((DEVICES, count), 0).astype(F32) == target
    rows = jnp.zeros((DEVICES, LANES), F32)
    for slot in range(SHOT_CAP):
        chosen = jnp.where(jnp.logical_and(owned, rank == slot), 1.0, 0.0).astype(BF16)
        held = jnp.where(lane // 5 == slot, record, 0.0).astype(BF16)
        rows = rows + jnp.dot(chosen, held, preferred_element_type=F32)
    return rows.astype(BF16)


def pack_images(swap, images_ref, out_ref):
    count = images_ref.shape[0]
    for band in range(PACK_ROWS // 16):
        for group in range(count // 16):
            block = images_ref[group * 16 : group * 16 + 16, band * 16 : band * 16 + 16]
            turned = jnp.dot(
                swap, block.reshape(256, TILE), preferred_element_type=F32
            ).astype(BF16)
            for r in range(16):
                for half in range(TILE // LANES):
                    place = ((r % 2) * 2 + half) * count + group * 16
                    out_ref[band * 8 + r // 2, place : place + 16, :] = turned[
                        r * 16 : r * 16 + 16, half * LANES : half * LANES + LANES
                    ]


def pack_rest_kernel(images_ref, out_ref):
    pack_images(swap_matrix(), images_ref, out_ref)


def pack_kernel(
    images_ref, heights_ref, shadow_ref, table_ref, shots_ref,
    out_ref, split_ref, extra_ref, halves_ref,
):
    step = pl.program_id(0)
    swap = swap_matrix()

    @pl.when(step == 0)
    def start():
        tiles = []
        for source, kind in ((heights_ref, 0), (shadow_ref, 1)):
            parts = []
            for half in range(2):
                lanes = slice(half * LANES, half * LANES + LANES)
                block = source[:, lanes]
                halves_ref[kind * 2 + half] = block if kind == 0 else 1.0 - block.astype(F32)
            for side in range(2):
                parts.append(
                    jnp.concatenate(
                        [halves_ref[kind * 2 + half, pl.ds(side, DEVICES, 2), :] for half in range(2)],
                        axis=1,
                    )
                )
            tiles.append(parts)
        (even, odd), (lit_even, lit_odd) = tiles
        split_ref[:DEVICES] = even
        split_ref[DEVICES:] = odd
        first = around_pieces(even, odd)
        lit = jnp.concatenate([lit_even, lit_odd], axis=1).astype(BF16)
        table = table_ref[...].astype(BF16)
        second = [lit[:, j * LANES : j * LANES + LANES] for j in range(4)]
        second += [jnp.broadcast_to(table[j : j + 1], (DEVICES, LANES)) for j in range(3)]
        second += [shot_rows(shots_ref[...])] + [jnp.zeros((DEVICES, LANES), BF16)] * 8
        for group in range(DEVICES // 16):
            span = slice(group * 16, group * 16 + 16)
            extra_ref[span, 0:16] = swapped(swap, [item[span] for item in first])
            extra_ref[span, 16:32] = swapped(swap, [item[span] for item in second])

    pack_images(swap, images_ref, out_ref)
    per_step = PACK_ROWS // 2
    here = pl.ds(pl.multiple_of(step * per_step, per_step), per_step)
    pixel_rows = QUARTERS * images_ref.shape[0]
    out_ref[:, pixel_rows : pixel_rows + EXTRA, :] = extra_ref[here, 0:EXTRA, :]


def pack(images, heights, shadow, table, shots):
    per_step = PACK_ROWS // 2
    count = PARTS[0][1]
    rows = QUARTERS * count + EXTRA
    whole = lambda s: (0, 0)
    return pl.pallas_call(
        pack_kernel,
        grid=(DEVICES // per_step,),
        in_specs=[
            pl.BlockSpec((count, PACK_ROWS, TILE), lambda s: (0, s, 0)),
            pl.BlockSpec((TILE, TILE), whole),
            pl.BlockSpec((TILE, TILE), whole),
            pl.BlockSpec((8, LANES), whole),
            pl.BlockSpec((8, TILE), whole),
        ],
        out_specs=[
            pl.BlockSpec((per_step, rows, LANES), lambda s: (s, 0, 0)),
            pl.BlockSpec((TILE, TILE), whole),
        ],
        out_shape=[
            jax.ShapeDtypeStruct((DEVICES, rows, LANES), BF16),
            jax.ShapeDtypeStruct((TILE, TILE), F32),
        ],
        scratch_shapes=[
            pltpu.VMEM((DEVICES, 32, LANES), BF16),
            pltpu.VMEM((4, TILE, LANES), F32),
        ],
        compiler_params=pltpu.CompilerParams(vmem_limit_bytes=58 * 1024 * 1024),
    )(images, heights, shadow, table, shots)


def pack_rest(images):
    per_step = PACK_ROWS // 2
    start, count = PARTS[1]
    rows = QUARTERS * count
    return pl.pallas_call(
        pack_rest_kernel,
        grid=(DEVICES // per_step,),
        in_specs=[pl.BlockSpec((count, PACK_ROWS, TILE), lambda s: (start // count, s, 0))],
        out_specs=pl.BlockSpec((per_step, rows, LANES), lambda s: (s, 0, 0)),
        out_shape=jax.ShapeDtypeStruct((DEVICES, rows, LANES), BF16),
        compiler_params=pltpu.CompilerParams(vmem_limit_bytes=58 * 1024 * 1024),
        cost_estimate=pl.CostEstimate(
            flops=2 * 256 * TILE * TILE * count, bytes_accessed=4 * TILE * TILE * count, transcendentals=0
        ),
    )(images)


SUM_SRC = (32, 64)
WIDTH = 2 * SLAB + TILE


def sideways(value):
    lane = iota_of(value.shape, 1)
    column = iota_of(value.shape, 0) % N_COL
    before = pltpu.roll(value, 1, 1)
    first = jnp.where(column == 0, 0.0, pltpu.roll(before, 1, 0))
    after = pltpu.roll(value, TILE - 1, 1)
    last = jnp.where(column == N_COL - 1, 0.0, pltpu.roll(after, DEVICES - 1, 0))
    return jnp.where(lane == 0, first, before), jnp.where(lane == TILE - 1, last, after)


def central_x(value):
    before, after = sideways(value)
    return after - before


def shift_tiles(value, count):
    pad = jnp.zeros((abs(count),) + value.shape[1:], value.dtype)
    if count > 0:
        return jnp.concatenate([pad, value[:-count]], axis=0)
    return jnp.concatenate([value[-count:], pad], axis=0)


def slab_normals(me, around_ref, lit_ref, normal_ref, slopes_ref, rows_ref):
    swap = swap_matrix()
    for group in range(DEVICES // 16):
        span = slice(group * 16, group * 16 + 16)
        turned = jnp.dot(
            swap, around_ref[span].reshape(256, LANES), preferred_element_type=F32
        )
        fine = turned[:128] + turned[128:]
        for r in range(4):
            for half in range(2):
                at = (2 * r + half) * 16
                rows_ref[r, span, half * LANES : half * LANES + LANES] = fine[at : at + 16]
    rows = [rows_ref[r] for r in range(4)]
    top = jnp.where(me == 0, shift_tiles(rows[0], N_COL), rows[0])
    bottom = jnp.where(me == DEVICES - 1, shift_tiles(rows[3], -N_COL), rows[3])
    slope_x = jnp.concatenate([central_x(rows[1]), central_x(rows[2])], axis=1) * 0.5
    slope_y = jnp.concatenate([rows[2] - top, bottom - rows[1]], axis=1) * 0.5
    inverse = lax.rsqrt(1.0 + slope_x * slope_x + slope_y * slope_y)
    slopes_ref[0], slopes_ref[1], slopes_ref[2] = slope_x, slope_y, inverse
    scale = 0.5 * sharpness
    x_head, x_tail = two_terms(-slope_x * inverse * scale)
    y_head, y_tail = two_terms(-slope_y * inverse * scale)
    steep = ((inverse - 1.0) * scale).astype(BF16)
    flat = jnp.where(lit_ref[...] > 0.5, scale, -2048.0).astype(BF16)
    for place, item in enumerate((x_head, y_head, x_tail, y_tail, steep, flat)):
        normal_ref[place * DEVICES : (place + 1) * DEVICES] = item


def slab_reply(me, lit_ref, slopes_ref, sums_ref, plain_ref, reply_ref):
    lit = lit_ref[...]
    slope_x, slope_y, inverse = slopes_ref[0], slopes_ref[1], slopes_ref[2]
    cube = inverse * inverse * inverse
    lane = iota_of((16, LANES), 1)
    scalars = jnp.zeros((16, LANES), BF16)
    totals = []
    for part in range(2):
        value = jnp.sum(plain_ref[:, part * SLAB : (part + 1) * SLAB], keepdims=True)
        total = jnp.zeros((1, 1), F32)
        for term in range(3):
            head = value.astype(BF16).astype(F32)
            scalars = jnp.where(lane == part * 3 + term, head, scalars.astype(F32)).astype(BF16)
            value = value - head
            total = total + head
        totals.append(total)
    guess = own_albedo(totals[0], totals[1])
    fields = []
    for part in range(2):
        by_x, by_y, by_z = (
            sums_ref[j * DEVICES : (j + 1) * DEVICES, part * SLAB : (part + 1) * SLAB]
            for j in range(3)
        )
        turned = (by_z - slope_x * by_x - slope_y * by_y) * cube
        grad_x = -lit * (by_x * inverse + slope_x * turned)
        grad_y = -lit * (by_y * inverse + slope_y * turned)
        across = jnp.concatenate([central_x(grad_x[:, :TILE]), central_x(grad_x[:, TILE:])], axis=1)
        halo = jnp.where(
            me == 0, shift_tiles(grad_y[:, :TILE], -N_COL), shift_tiles(grad_y[:, TILE:], N_COL)
        )
        fields.append(jnp.concatenate([across * (-0.5), grad_y, halo], axis=1))
    seen, model = fields
    flat = jnp.concatenate([model.astype(BF16), (guess * model - seen).astype(BF16)], axis=1)
    swap, short_swap = swap_matrix(), swap_matrix(8, 16)
    for group in range(DEVICES // 16):
        span = slice(group * 16, group * 16 + 16)
        pieces = [flat[span, j * LANES : (j + 1) * LANES] for j in range(20)]
        pieces = pieces + [scalars] + [jnp.zeros((16, LANES), BF16)] * 3
        reply_ref[span, 0:16, :] = swapped(swap, pieces[:16])
        reply_ref[span, 16:24, :] = swapped(short_swap, pieces[16:])


def sum_images(part, meta_ref, pixels_ref, normal_ref, sums_ref, plain_ref, work):
    first_w, second_w, first_p, second_p = work
    count = PARTS[part][1]
    half_src = SUM_SRC[part] // 2
    half_img = half_src * count

    def front(side, w_ref, p_ref):
        meta = meta_ref[:, side * half_img : (side + 1) * half_img]
        cols = meta.T
        hot = iota_of((half_img, DEVICES), 1).astype(F32) == cols[:, 0:1]
        sun = [jnp.where(hot, cols[:, j : j + 1], 0.0).astype(BF16) for j in (1, 2, 3)]
        pick = jnp.concatenate([sun[0], sun[1], sun[0], sun[1], sun[2], sun[2]], axis=1)
        hot_t = iota_of((DEVICES, half_img), 0).astype(F32) == meta[0:1, :]
        for j in range(3):
            p_ref[j * DEVICES : (j + 1) * DEVICES] = jnp.where(
                hot_t, meta[j + 1 : j + 2, :], 0.0
            ).astype(BF16)
        chunks = half_img // (192 if count == 48 else 128)
        few, images = (half_src // chunks, half_img // chunks)
        for chunk in range(chunks):
            span = slice(chunk * images, (chunk + 1) * images)
            src = slice(side * half_src + chunk * few, side * half_src + (chunk + 1) * few)
            half_angle = jnp.dot(pick[span], normal_ref[...], preferred_element_type=F32)
            gain = cols[span, 4:5]
            bend = jnp.tanh(half_angle)
            refl = (jnp.log(1.0 - bend) - LOG_2) * (gain * (-1.0 / sharpness))
            sigma = bend * (gain * 0.5) + gain * 0.5
            seen = jnp.concatenate(
                [
                    pixels_ref[src, q * count : q * count + count, :].reshape(images, LANES)
                    for q in range(QUARTERS)
                ],
                axis=1,
            ).astype(F32)
            w_ref[span, :SLAB] = (seen * sigma).astype(BF16)
            w_ref[span, SLAB:] = (refl * sigma).astype(BF16)
            plain_ref[:, :SLAB] += jnp.sum((seen * refl).reshape(-1, 8, SLAB), axis=0)
            plain_ref[:, SLAB:] += jnp.sum((refl * refl).reshape(-1, 8, SLAB), axis=0)

    def back(w_ref, p_ref):
        sums_ref[...] += jnp.dot(p_ref[...], w_ref[...], preferred_element_type=F32)

    @pl.when(pl.program_id(0) == 0)
    def start():
        second_w[...] = jnp.zeros_like(second_w)
        second_p[...] = jnp.zeros_like(second_p)

    back(second_w, second_p)
    front(0, first_w, first_p)
    back(first_w, first_p)
    front(1, second_w, second_p)

    @pl.when(pl.program_id(0) == pl.num_programs(0) - 1)
    def finish():
        back(second_w, second_p)


def first_kernel(
    me_ref, meta_ref, pixels_ref, around_ref, lit_ref,
    sums_ref, plain_ref, normal_ref, slopes_ref, rows_ref, *work,
):
    @pl.when(pl.program_id(0) == 0)
    def start():
        sums_ref[...] = jnp.zeros_like(sums_ref)
        plain_ref[...] = jnp.zeros_like(plain_ref)
        slab_normals(me_ref[0], around_ref, lit_ref, normal_ref, slopes_ref, rows_ref)

    sum_images(0, meta_ref, pixels_ref, normal_ref, sums_ref, plain_ref, work)


def second_kernel(
    me_ref, meta_ref, pixels_ref, around_ref, lit_ref, sums_in, plain_in,
    reply_ref, sums_ref, plain_ref, normal_ref, slopes_ref, rows_ref, *work,
):
    @pl.when(pl.program_id(0) == 0)
    def start():
        sums_ref[...] = sums_in[...]
        plain_ref[...] = plain_in[...]
        slab_normals(me_ref[0], around_ref, lit_ref, normal_ref, slopes_ref, rows_ref)

    sum_images(1, meta_ref, pixels_ref, normal_ref, sums_ref, plain_ref, work)

    @pl.when(pl.program_id(0) == pl.num_programs(0) - 1)
    def finish():
        slab_reply(me_ref[0], lit_ref, slopes_ref, sums_ref, plain_ref, reply_ref)


SUMS = ((3 * DEVICES, 2 * SLAB), F32)
PLAIN = ((8, 2 * SLAB), F32)
NORMALS = ((6 * DEVICES, SLAB), BF16)
SLOPES = ((3, DEVICES, SLAB), F32)
ROWS = ((4, DEVICES, TILE), F32)


def kept(shape):
    return pl.BlockSpec(shape, lambda s: (0,) * len(shape))


def sum_call(part, kernel, inputs, specs, outs, scratch):
    count, sources = PARTS[part][1], SUM_SRC[part]
    half = sources * count // 2
    rows = QUARTERS * count + (EXTRA if part == 0 else 0)
    cells = DEVICES * count * SLAB
    return pl.pallas_call(
        kernel,
        grid=(DEVICES // sources,),
        in_specs=[
            pl.BlockSpec(memory_space=pltpu.SMEM),
            pl.BlockSpec((8, sources * count), lambda s: (0, s)),
            pl.BlockSpec((sources, rows, LANES), lambda s: (s, 0, 0)),
        ]
        + specs,
        out_specs=[kept(shape) for shape, dtype in outs],
        out_shape=[jax.ShapeDtypeStruct(shape, dtype) for shape, dtype in outs],
        scratch_shapes=[pltpu.VMEM(shape, dtype) for shape, dtype in scratch]
        + [pltpu.VMEM((half, 2 * SLAB), BF16)] * 2
        + [pltpu.VMEM((3 * DEVICES, half), BF16)] * 2,
        compiler_params=pltpu.CompilerParams(vmem_limit_bytes=44 * 1024 * 1024),
        cost_estimate=pl.CostEstimate(
            flops=2 * 12 * DEVICES * cells, bytes_accessed=4 * cells, transcendentals=2 * cells
        ),
    )(*inputs)


def first_sums(me, meta, pixels, around, lit):
    return sum_call(
        0,
        first_kernel,
        (me, meta, pixels, around, lit),
        [kept((DEVICES, 16, LANES)), kept((DEVICES, SLAB))],
        (SUMS, PLAIN),
        (NORMALS, SLOPES, ROWS),
    )


def second_sums(me, meta, pixels, around, lit, sums, plain):
    return sum_call(
        1,
        second_kernel,
        (me, meta, pixels, around, lit, sums, plain),
        [kept((DEVICES, 16, LANES)), kept((DEVICES, SLAB)), kept(SUMS[0]), kept(PLAIN[0])],
        (((DEVICES, REPLY, LANES), BF16),),
        (SUMS, PLAIN, NORMALS, SLOPES, ROWS),
    )[0]


def owner_kernel(final, *refs):
    got_ref, surface_ref, hits_ref, height_ref, ends_ref, sides_ref = refs[:6]
    outs, (model_ref, misfit_ref, scalar_ref, mixed_ref) = refs[6:-4], refs[-4:]
    swap, short_swap = swap_matrix(), swap_matrix(16, 8)
    for group in range(DEVICES // 16):
        span = slice(group * 16, group * 16 + 16)
        rows = []
        for matrix, start, count in ((swap, 0, 16), (short_swap, 16, 8)):
            block = got_ref[span, start : start + count, :].reshape(16 * count, LANES)
            turned = jnp.dot(matrix, block, preferred_element_type=F32)
            rows += [turned[j * 16 : j * 16 + 16] for j in range(count)]
        for j in range(10):
            model_ref[j, span] = rows[j]
            misfit_ref[j, span] = rows[10 + j]
        scalar_ref[span] = rows[20]
    scalars = scalar_ref[...]
    cross = scalars[:, 0:1] + scalars[:, 1:2] + scalars[:, 2:3]
    power = scalars[:, 3:4] + scalars[:, 4:5] + scalars[:, 5:6]
    albedo = jnp.sum(cross, keepdims=True) / jnp.sum(power, keepdims=True)
    rest = albedo * (albedo - own_albedo(cross, power))

    def grad(j):
        return jnp.concatenate(
            [albedo * misfit_ref[i] + rest * model_ref[i] for i in (j, j + 1)], axis=1
        )

    row = iota_of((DEVICES, TILE), 0)
    lane = iota_of((DEVICES, TILE), 1)
    along_even, along_odd, halo = grad(4), grad(6), grad(8)
    before = jnp.where(row == 0, pltpu.roll(halo, 1, 0), pltpu.roll(along_odd, 1, 0))
    after = jnp.where(
        row == DEVICES - 1,
        pltpu.roll(halo, DEVICES - 1, 0),
        pltpu.roll(along_even, DEVICES - 1, 0),
    )
    data = (grad(0) + (before - along_odd) * 0.5, grad(2) + (along_even - after) * 0.5)
    old = (surface_ref[:DEVICES], surface_ref[DEVICES:])
    above = jnp.where(row == 0, ends_ref[0:1], pltpu.roll(old[1], 1, 0))
    below = jnp.where(row == DEVICES - 1, ends_ref[1:2], pltpu.roll(old[0], DEVICES - 1, 0))
    vertical = (above + old[1], old[0] + below)
    new = []
    for part in range(2):
        span = slice(part * DEVICES, (part + 1) * DEVICES)
        left = jnp.where(lane == 0, sides_ref[span, 0:1], pltpu.roll(old[part], 1, 1))
        right = jnp.where(
            lane == TILE - 1, sides_ref[span, 1:2], pltpu.roll(old[part], TILE - 1, 1)
        )
        laplace = vertical[part] + left + right - 4.0 * old[part]
        laser = hits_ref[span] * old[part] - height_ref[span]
        new.append(
            old[part]
            - step_size * (data[part] - smooth_weight * laplace + laser_weight * laser)
        )
    if final:
        for part in range(2):
            for half in range(2):
                lanes = slice(half * LANES, half * LANES + LANES)
                mixed_ref[pl.ds(half * TILE + part, DEVICES, 2), :] = new[part][:, lanes]
        for half in range(2):
            outs[0][:, half * LANES : half * LANES + LANES] = mixed_ref[
                half * TILE : half * TILE + TILE
            ]
        return
    outs[0][:DEVICES], outs[0][DEVICES:] = new[0], new[1]
    pieces = around_pieces(new[0], new[1])
    for group in range(DEVICES // 16):
        span = slice(group * 16, group * 16 + 16)
        outs[1][span] = swapped(swap, [item[span] for item in pieces])


def owner_update(final, got, surface, hits, height_sum, rims):
    above, below, left, right = rims
    ends = jnp.concatenate([above, below], axis=0)
    sides = jnp.concatenate([left, right], axis=1)
    out_shape = [jax.ShapeDtypeStruct((TILE, TILE), F32)]
    if not final:
        out_shape.append(jax.ShapeDtypeStruct((DEVICES, 16, LANES), BF16))
    return pl.pallas_call(
        functools.partial(owner_kernel, final),
        out_shape=out_shape,
        scratch_shapes=[
            pltpu.VMEM((10, DEVICES, LANES), F32),
            pltpu.VMEM((10, DEVICES, LANES), F32),
            pltpu.VMEM((DEVICES, LANES), F32),
            pltpu.VMEM((2 * TILE, LANES), F32),
        ],
        compiler_params=pltpu.CompilerParams(vmem_limit_bytes=32 * 1024 * 1024),
    )(got, surface, hits, height_sum, ends, sides)


def shot_sums(slots):
    cell = lax.broadcasted_iota(jnp.int32, (1, TILE), 1).astype(F32)
    present = slots[:, 4:5]
    in_row = jnp.where(slots[:, 0:1] == cell, 1.0, 0.0)
    in_col = jnp.where(slots[:, 1:2] == cell, 1.0, 0.0).astype(BF16)
    left = jnp.concatenate([in_row * slots[:, j : j + 1] * present for j in (4, 2, 3)], axis=1)
    both = lax.dot_general(
        left.astype(BF16), in_col, (((0,), (0,)), ((), ())), preferred_element_type=F32
    )
    return both[:TILE], both[TILE : 2 * TILE] + both[2 * TILE :]


def body(heights, shadow, image_tiles, image_dest, sun_gain, shot_dest, shot_pixel, shot_height):
    me = (lax.axis_index("row") * N_COL + lax.axis_index("col")).astype(jnp.int32)[None]
    dest = image_dest[:, 0].astype(F32)
    table = jnp.concatenate([dest, jnp.zeros_like(dest), sun_gain.astype(F32).T.reshape(-1)])
    table = jnp.pad(table.reshape(3, LANES), ((0, 5), (0, 0)))
    shots = jnp.stack([shot_dest[:, 0].astype(F32), shot_pixel.astype(F32), shot_height])
    shots = jnp.pad(shots, ((0, 5), (0, 0)))
    packed, surface = pack(image_tiles, heights, shadow, table, shots)
    rims = edges(surface)
    pixels = (exchange(packed), exchange(pack_rest(image_tiles)))
    extra = pixels[0][:, QUARTERS * PARTS[0][1] :, :]
    metas = []
    for start, count in PARTS:
        lists = [
            extra[:, row, at + start : at + start + count]
            for row, at in ((20, 0), (21, 0), (21, IMG), (22, 0), (22, IMG))
        ]
        meta = jnp.stack(lists).astype(F32).reshape(5, DEVICES * count)
        metas.append(jnp.pad(meta, ((0, 3), (0, 0))))
    slab_lit = extra[:, 16:20, :].reshape(DEVICES, SLAB).astype(F32)
    around = extra[:, 0:16, :]
    slots = extra[:, 23, : SHOT_CAP * 5].reshape(DEVICES * SHOT_CAP, 5).astype(F32)
    hits, height_sum = shot_sums(slots)

    def slab_pass(around):
        begun = first_sums(me, metas[0], pixels[0], around, slab_lit)
        return second_sums(me, metas[1], pixels[1], around, slab_lit, *begun)

    got = exchange(slab_pass(around))
    surface, around = owner_update(False, got, surface, hits, height_sum, rims)
    around = exchange(around)
    rims = edges(surface)
    got = exchange(slab_pass(around))
    return owner_update(True, got, surface, hits, height_sum, rims)[0]


def solution(mesh):
    placed = (
        P("row", "col"),
        P("row", "col"),
        P(("row", "col"), None, None),
        P(("row", "col"), None),
        P(("row", "col"), None),
        P(("row", "col"), None),
        P(("row", "col")),
        P(("row", "col")),
    )
    return jax.shard_map(
        body, mesh=mesh, in_specs=placed, out_specs=P("row", "col"), check_vma=False
    )
```

```python
import functools

import jax
import jax.numpy as jnp
from jax import lax
from jax.experimental import pallas as pl
from jax.experimental.pallas import tpu as pltpu
from jax.sharding import PartitionSpec as P

sharpness = 8.0
step_size = 0.01
smooth_weight = 2.0
laser_weight = 20.0

AXES = ("row", "col")
DEVICES = 128
N_COL = 16
TILE = 256
IMG = 64
SLAB = 512
LANES = 128
QUARTERS = SLAB // LANES
PARTS = ((0, 48), (48, 16))
EXTRA = 24
REPLY = 24
SHOT_CAP = 4
LOG_2 = 0.6931471805599453
F32 = jnp.float32
BF16 = jnp.bfloat16


def exchange(value):
    return lax.all_to_all(value, AXES, split_axis=0, concat_axis=0, tiled=True)


def edges(value):
    out = []
    for axis, dim in (("row", 0), ("col", 1)):
        devices, length = (lax.axis_size(axis), value.shape[dim])
        up = [(i, (i + 1) % devices) for i in range(devices - 1)]
        down = [(j, i) for i, j in up]
        last = lax.slice_in_dim(value, length - 1, length, axis=dim)
        first = lax.slice_in_dim(value, 0, 1, axis=dim)
        out.append(lax.ppermute(last, axis, up))
        out.append(lax.ppermute(first, axis, down))
    return out


def own_albedo(cross, power):
    return jnp.where(power > 0.0, cross / jnp.where(power > 0.0, power, 1.0), 0.0)


PACK_ROWS = 64


def swap_matrix(blocks=16, rows=16):
    to = lax.broadcasted_iota(jnp.int32, (blocks * rows, blocks * rows), 0)
    source = lax.broadcasted_iota(jnp.int32, (blocks * rows, blocks * rows), 1)
    return jnp.where((to % blocks) * rows + to // blocks == source, 1.0, 0.0).astype(BF16)


def iota_of(shape, dim):
    return lax.broadcasted_iota(jnp.int32, shape, dim)


def two_terms(value):
    head = value.astype(BF16)
    return head, (value - head.astype(F32)).astype(BF16)


def swapped(swap, pieces):
    turned = jnp.dot(swap, jnp.concatenate(pieces, axis=0), preferred_element_type=F32)
    return turned.astype(BF16).reshape(16, len(pieces), LANES)


def around_pieces(even, odd):
    four = (pltpu.roll(odd, 1, 0), even, odd, pltpu.roll(even, DEVICES - 1, 0))
    terms = [two_terms(item) for item in four]
    return [
        terms[r][term][:, half * LANES : half * LANES + LANES]
        for term in range(2)
        for r in range(4)
        for half in range(2)
    ]


def shot_rows(target, pixel, height):
    count = target.shape[1]
    head = height.astype(BF16).astype(F32)
    grid_row = jnp.floor(pixel * (1.0 / TILE))
    pair = jnp.floor(grid_row * 0.5)
    columns = jnp.concatenate(
        [
            target,
            (grid_row - 2.0 * pair) * DEVICES + pair,
            pixel - TILE * grid_row,
            head,
            height - head,
            jnp.ones_like(height),
            jnp.zeros((2, count), F32),
        ],
        axis=0,
    ).T
    alike = columns[:, 0:1] == target
    before = iota_of((count, count), 0) < iota_of((count, count), 1)
    rank = jnp.sum(jnp.where(jnp.logical_and(alike, before), 1.0, 0.0), axis=0, keepdims=True)
    lane = iota_of((count, LANES), 1)
    record = jnp.zeros((count, LANES), F32)
    for member in range(5):
        record = jnp.where(lane % 5 == member, columns[:, member + 1 : member + 2], record)
    owned = iota_of((DEVICES, count), 0).astype(F32) == target
    rows = jnp.zeros((DEVICES, LANES), F32)
    for slot in range(SHOT_CAP):
        chosen = jnp.where(jnp.logical_and(owned, rank == slot), 1.0, 0.0).astype(BF16)
        held = jnp.where(lane // 5 == slot, record, 0.0).astype(BF16)
        rows = rows + jnp.dot(chosen, held, preferred_element_type=F32)
    return rows.astype(BF16)


def pack_images(swap, images_ref, out_ref):
    count = images_ref.shape[0]
    for band in range(PACK_ROWS // 16):
        for group in range(count // 16):
            block = images_ref[group * 16 : group * 16 + 16, band * 16 : band * 16 + 16]
            turned = jnp.dot(
                swap, block.reshape(256, TILE), preferred_element_type=F32
            ).astype(BF16)
            for r in range(16):
                for half in range(TILE // LANES):
                    place = ((r % 2) * 2 + half) * count + group * 16
                    out_ref[band * 8 + r // 2, place : place + 16, :] = turned[
                        r * 16 : r * 16 + 16, half * LANES : half * LANES + LANES
                    ]


def pack_rest_kernel(images_ref, out_ref):
    pack_images(swap_matrix(), images_ref, out_ref)


def pack_kernel(
    images_ref, heights_ref, shadow_ref, dest_ref, sun_ref, shot_dest_ref, pixel_ref, shot_height_ref,
    out_ref, split_ref, extra_ref, halves_ref,
):
    step = pl.program_id(0)
    swap = swap_matrix()

    @pl.when(step == 0)
    def start():
        tiles = []
        for source, kind in ((heights_ref, 0), (shadow_ref, 1)):
            parts = []
            for half in range(2):
                lanes = slice(half * LANES, half * LANES + LANES)
                block = source[:, lanes]
                halves_ref[kind * 2 + half] = block if kind == 0 else 1.0 - block.astype(F32)
            for side in range(2):
                parts.append(
                    jnp.concatenate(
                        [halves_ref[kind * 2 + half, pl.ds(side, DEVICES, 2), :] for half in range(2)],
                        axis=1,
                    )
                )
            tiles.append(parts)
        (even, odd), (lit_even, lit_odd) = tiles
        split_ref[:DEVICES] = even
        split_ref[DEVICES:] = odd
        first = around_pieces(even, odd)
        lit = jnp.concatenate([lit_even, lit_odd], axis=1).astype(BF16)
        sun = sun_ref[...].astype(F32)
        dest = dest_ref[...].astype(F32)
        table = [
            jnp.concatenate([dest, jnp.zeros_like(dest)], axis=1),
            jnp.concatenate([sun[0:1], sun[1:2]], axis=1),
            jnp.concatenate([sun[2:3], sun[3:4]], axis=1),
        ]
        second = [lit[:, j * LANES : j * LANES + LANES] for j in range(4)]
        second += [jnp.broadcast_to(item, (DEVICES, LANES)).astype(BF16) for item in table]
        shots = (shot_dest_ref[...].astype(F32), pixel_ref[...].astype(F32), shot_height_ref[...])
        second += [shot_rows(*shots)] + [jnp.zeros((DEVICES, LANES), BF16)] * 8
        for group in range(DEVICES // 16):
            span = slice(group * 16, group * 16 + 16)
            extra_ref[span, 0:16] = swapped(swap, [item[span] for item in first])
            extra_ref[span, 16:32] = swapped(swap, [item[span] for item in second])

    pack_images(swap, images_ref, out_ref)
    per_step = PACK_ROWS // 2
    here = pl.ds(pl.multiple_of(step * per_step, per_step), per_step)
    pixel_rows = QUARTERS * images_ref.shape[0]
    out_ref[:, pixel_rows : pixel_rows + EXTRA, :] = extra_ref[here, 0:EXTRA, :]


def pack(images, heights, shadow, *small):
    per_step = PACK_ROWS // 2
    count = PARTS[0][1]
    rows = QUARTERS * count + EXTRA
    whole = lambda s: (0, 0)
    return pl.pallas_call(
        pack_kernel,
        grid=(DEVICES // per_step,),
        in_specs=[
            pl.BlockSpec((count, PACK_ROWS, TILE), lambda s: (0, s, 0)),
            pl.BlockSpec((TILE, TILE), whole),
            pl.BlockSpec((TILE, TILE), whole),
        ]
        + [pl.BlockSpec(item.shape, whole) for item in small],
        out_specs=[
            pl.BlockSpec((per_step, rows, LANES), lambda s: (s, 0, 0)),
            pl.BlockSpec((TILE, TILE), whole),
        ],
        out_shape=[
            jax.ShapeDtypeStruct((DEVICES, rows, LANES), BF16),
            jax.ShapeDtypeStruct((TILE, TILE), F32),
        ],
        scratch_shapes=[
            pltpu.VMEM((DEVICES, 32, LANES), BF16),
            pltpu.VMEM((4, TILE, LANES), F32),
        ],
        compiler_params=pltpu.CompilerParams(vmem_limit_bytes=58 * 1024 * 1024),
    )(images, heights, shadow, *small)


def pack_rest(images):
    per_step = PACK_ROWS // 2
    start, count = PARTS[1]
    rows = QUARTERS * count
    return pl.pallas_call(
        pack_rest_kernel,
        grid=(DEVICES // per_step,),
        in_specs=[pl.BlockSpec((count, PACK_ROWS, TILE), lambda s: (start // count, s, 0))],
        out_specs=pl.BlockSpec((per_step, rows, LANES), lambda s: (s, 0, 0)),
        out_shape=jax.ShapeDtypeStruct((DEVICES, rows, LANES), BF16),
        compiler_params=pltpu.CompilerParams(vmem_limit_bytes=58 * 1024 * 1024),
        cost_estimate=pl.CostEstimate(
            flops=2 * 256 * TILE * TILE * count, bytes_accessed=4 * TILE * TILE * count, transcendentals=0
        ),
    )(images)


SUM_SRC = (32, 64)
STEPS = (DEVICES // 32, DEVICES // 64)
WIDTH = 2 * SLAB + TILE


def sideways(value):
    lane = iota_of(value.shape, 1)
    column = iota_of(value.shape, 0) % N_COL
    before = pltpu.roll(value, 1, 1)
    first = jnp.where(column == 0, 0.0, pltpu.roll(before, 1, 0))
    after = pltpu.roll(value, TILE - 1, 1)
    last = jnp.where(column == N_COL - 1, 0.0, pltpu.roll(after, DEVICES - 1, 0))
    return jnp.where(lane == 0, first, before), jnp.where(lane == TILE - 1, last, after)


def central_x(value):
    before, after = sideways(value)
    return after - before


def shift_tiles(value, count):
    pad = jnp.zeros((abs(count),) + value.shape[1:], value.dtype)
    if count > 0:
        return jnp.concatenate([pad, value[:-count]], axis=0)
    return jnp.concatenate([value[-count:], pad], axis=0)


def slab_normals(me, around_ref, lit_ref, normal_ref, slopes_ref, rows_ref):
    swap = swap_matrix()
    for group in range(DEVICES // 16):
        span = slice(group * 16, group * 16 + 16)
        turned = jnp.dot(
            swap, around_ref[span].reshape(256, LANES), preferred_element_type=F32
        )
        fine = turned[:128] + turned[128:]
        for r in range(4):
            for half in range(2):
                at = (2 * r + half) * 16
                rows_ref[r, span, half * LANES : half * LANES + LANES] = fine[at : at + 16]
    rows = [rows_ref[r] for r in range(4)]
    top = jnp.where(me == 0, shift_tiles(rows[0], N_COL), rows[0])
    bottom = jnp.where(me == DEVICES - 1, shift_tiles(rows[3], -N_COL), rows[3])
    slope_x = jnp.concatenate([central_x(rows[1]), central_x(rows[2])], axis=1) * 0.5
    slope_y = jnp.concatenate([rows[2] - top, bottom - rows[1]], axis=1) * 0.5
    inverse = lax.rsqrt(1.0 + slope_x * slope_x + slope_y * slope_y)
    slopes_ref[0], slopes_ref[1], slopes_ref[2] = slope_x, slope_y, inverse
    scale = 0.5 * sharpness
    x_head, x_tail = two_terms(-slope_x * inverse * scale)
    y_head, y_tail = two_terms(-slope_y * inverse * scale)
    steep = ((inverse - 1.0) * scale).astype(BF16)
    flat = jnp.where(lit_ref[...] > 0.5, scale, -2048.0).astype(BF16)
    for place, item in enumerate((x_head, y_head, x_tail, y_tail, steep, flat)):
        normal_ref[place * DEVICES : (place + 1) * DEVICES] = item


def slab_reply(me, lit_ref, slopes_ref, sums_ref, plain_ref, reply_ref):
    lit = lit_ref[...]
    slope_x, slope_y, inverse = slopes_ref[0], slopes_ref[1], slopes_ref[2]
    cube = inverse * inverse * inverse
    lane = iota_of((16, LANES), 1)
    scalars = jnp.zeros((16, LANES), BF16)
    totals = []
    for part in range(2):
        value = jnp.sum(plain_ref[:, part * SLAB : (part + 1) * SLAB], keepdims=True)
        total = jnp.zeros((1, 1), F32)
        for term in range(3):
            head = value.astype(BF16).astype(F32)
            scalars = jnp.where(lane == part * 3 + term, head, scalars.astype(F32)).astype(BF16)
            value = value - head
            total = total + head
        totals.append(total)
    guess = own_albedo(totals[0], totals[1])
    fields = []
    for part in range(2):
        by_x, by_y, by_z = (
            sums_ref[j * DEVICES : (j + 1) * DEVICES, part * SLAB : (part + 1) * SLAB]
            for j in range(3)
        )
        turned = (by_z - slope_x * by_x - slope_y * by_y) * cube
        grad_x = -lit * (by_x * inverse + slope_x * turned)
        grad_y = -lit * (by_y * inverse + slope_y * turned)
        across = jnp.concatenate([central_x(grad_x[:, :TILE]), central_x(grad_x[:, TILE:])], axis=1)
        halo = jnp.where(
            me == 0, shift_tiles(grad_y[:, :TILE], -N_COL), shift_tiles(grad_y[:, TILE:], N_COL)
        )
        fields.append(jnp.concatenate([across * (-0.5), grad_y, halo], axis=1))
    seen, model = fields
    flat = jnp.concatenate([model.astype(BF16), (guess * model - seen).astype(BF16)], axis=1)
    swap, short_swap = swap_matrix(), swap_matrix(8, 16)
    for group in range(DEVICES // 16):
        span = slice(group * 16, group * 16 + 16)
        pieces = [flat[span, j * LANES : (j + 1) * LANES] for j in range(20)]
        pieces = pieces + [scalars] + [jnp.zeros((16, LANES), BF16)] * 3
        reply_ref[span, 0:16, :] = swapped(swap, pieces[:16])
        reply_ref[span, 16:24, :] = swapped(short_swap, pieces[16:])


def sum_images(part, step, steps, meta_ref, pixels_ref, normal_ref, sums_ref, plain_ref, work):
    first_w, second_w, first_p, second_p = work
    count = PARTS[part][1]
    half_src = SUM_SRC[part] // 2
    half_img = half_src * count

    def front(side, w_ref, p_ref):
        meta = meta_ref[:, side * half_img : (side + 1) * half_img]
        cols = meta.T
        hot = iota_of((half_img, DEVICES), 1).astype(F32) == cols[:, 0:1]
        sun = [jnp.where(hot, cols[:, j : j + 1], 0.0).astype(BF16) for j in (1, 2, 3)]
        pick = jnp.concatenate([sun[0], sun[1], sun[0], sun[1], sun[2], sun[2]], axis=1)
        hot_t = iota_of((DEVICES, half_img), 0).astype(F32) == meta[0:1, :]
        for j in range(3):
            p_ref[j * DEVICES : (j + 1) * DEVICES] = jnp.where(
                hot_t, meta[j + 1 : j + 2, :], 0.0
            ).astype(BF16)
        chunks = half_img // (192 if count == 48 else 128)
        few, images = (half_src // chunks, half_img // chunks)
        for chunk in range(chunks):
            span = slice(chunk * images, (chunk + 1) * images)
            src = slice(side * half_src + chunk * few, side * half_src + (chunk + 1) * few)
            half_angle = jnp.dot(pick[span], normal_ref[...], preferred_element_type=F32)
            gain = cols[span, 4:5]
            bend = jnp.tanh(half_angle)
            refl = (jnp.log2(1.0 - bend) - 1.0) * (gain * (-LOG_2 / sharpness))
            sigma = bend * (gain * 0.5) + gain * 0.5
            seen = jnp.concatenate(
                [
                    pixels_ref[src, q * count : q * count + count, :].reshape(images, LANES)
                    for q in range(QUARTERS)
                ],
                axis=1,
            ).astype(F32)
            w_ref[span, :SLAB] = (seen * sigma).astype(BF16)
            w_ref[span, SLAB:] = (refl * sigma).astype(BF16)
            plain_ref[:, :SLAB] += jnp.sum((seen * refl).reshape(-1, 8, SLAB), axis=0)
            plain_ref[:, SLAB:] += jnp.sum((refl * refl).reshape(-1, 8, SLAB), axis=0)

    def back(w_ref, p_ref):
        sums_ref[...] += jnp.dot(p_ref[...], w_ref[...], preferred_element_type=F32)

    @pl.when(step == 0)
    def start():
        second_w[...] = jnp.zeros_like(second_w)
        second_p[...] = jnp.zeros_like(second_p)

    back(second_w, second_p)
    front(0, first_w, first_p)
    back(first_w, first_p)
    front(1, second_w, second_p)

    @pl.when(step == steps - 1)
    def finish():
        back(second_w, second_p)


def first_kernel(
    me_ref, meta_ref, pixels_ref, around_ref, lit_ref,
    sums_ref, plain_ref, normal_ref, slopes_ref, rows_ref, *work,
):
    @pl.when(pl.program_id(0) == 0)
    def start():
        sums_ref[...] = jnp.zeros_like(sums_ref)
        plain_ref[...] = jnp.zeros_like(plain_ref)
        slab_normals(me_ref[0], around_ref, lit_ref, normal_ref, slopes_ref, rows_ref)

    sum_images(
        0, pl.program_id(0), STEPS[0], meta_ref, pixels_ref, normal_ref, sums_ref, plain_ref, work
    )


def second_kernel(
    me_ref, meta_ref, pixels_ref, around_ref, lit_ref, sums_in, plain_in,
    reply_ref, sums_ref, plain_ref, normal_ref, slopes_ref, rows_ref, *work,
):
    @pl.when(pl.program_id(0) == 0)
    def start():
        sums_ref[...] = sums_in[...]
        plain_ref[...] = plain_in[...]
        slab_normals(me_ref[0], around_ref, lit_ref, normal_ref, slopes_ref, rows_ref)

    sum_images(
        1, pl.program_id(0), STEPS[1], meta_ref, pixels_ref, normal_ref, sums_ref, plain_ref, work
    )

    @pl.when(pl.program_id(0) == pl.num_programs(0) - 1)
    def finish():
        slab_reply(me_ref[0], lit_ref, slopes_ref, sums_ref, plain_ref, reply_ref)


SUMS = ((3 * DEVICES, 2 * SLAB), F32)
PLAIN = ((8, 2 * SLAB), F32)
NORMALS = ((6 * DEVICES, SLAB), BF16)
SLOPES = ((3, DEVICES, SLAB), F32)
ROWS = ((4, DEVICES, TILE), F32)


def kept(shape):
    return pl.BlockSpec(shape, lambda s: (0,) * len(shape))


def sum_call(part, kernel, inputs, specs, outs, scratch):
    count, sources = PARTS[part][1], SUM_SRC[part]
    half = sources * count // 2
    rows = QUARTERS * count + (EXTRA if part == 0 else 0)
    cells = DEVICES * count * SLAB
    return pl.pallas_call(
        kernel,
        grid=(DEVICES // sources,),
        in_specs=[
            pl.BlockSpec(memory_space=pltpu.SMEM),
            pl.BlockSpec((8, sources * count), lambda s: (0, s)),
            pl.BlockSpec((sources, rows, LANES), lambda s: (s, 0, 0)),
        ]
        + specs,
        out_specs=[kept(shape) for shape, dtype in outs],
        out_shape=[jax.ShapeDtypeStruct(shape, dtype) for shape, dtype in outs],
        scratch_shapes=[pltpu.VMEM(shape, dtype) for shape, dtype in scratch]
        + [pltpu.VMEM((half, 2 * SLAB), BF16)] * 2
        + [pltpu.VMEM((3 * DEVICES, half), BF16)] * 2,
        compiler_params=pltpu.CompilerParams(vmem_limit_bytes=44 * 1024 * 1024),
        cost_estimate=pl.CostEstimate(
            flops=2 * 12 * DEVICES * cells, bytes_accessed=4 * cells, transcendentals=2 * cells
        ),
    )(*inputs)


def first_sums(me, meta, pixels, around, lit):
    return sum_call(
        0,
        first_kernel,
        (me, meta, pixels, around, lit),
        [kept((DEVICES, 16, LANES)), kept((DEVICES, SLAB))],
        (SUMS, PLAIN),
        (NORMALS, SLOPES, ROWS),
    )


def second_sums(me, meta, pixels, around, lit, sums, plain):
    return sum_call(
        1,
        second_kernel,
        (me, meta, pixels, around, lit, sums, plain),
        [kept((DEVICES, 16, LANES)), kept((DEVICES, SLAB)), kept(SUMS[0]), kept(PLAIN[0])],
        (((DEVICES, REPLY, LANES), BF16),),
        (SUMS, PLAIN, NORMALS, SLOPES, ROWS),
    )[0]


def both_kernel(
    me_ref, meta_ref, pixels_ref, meta_rest, pixels_rest, around_ref, lit_ref,
    reply_ref, sums_ref, plain_ref, normal_ref, slopes_ref, rows_ref, *work,
):
    step = pl.program_id(0)

    @pl.when(step == 0)
    def start():
        sums_ref[...] = jnp.zeros_like(sums_ref)
        plain_ref[...] = jnp.zeros_like(plain_ref)
        slab_normals(me_ref[0], around_ref, lit_ref, normal_ref, slopes_ref, rows_ref)

    @pl.when(step < STEPS[0])
    def first():
        sum_images(
            0, step, STEPS[0], meta_ref, pixels_ref, normal_ref, sums_ref, plain_ref, work[:4]
        )

    @pl.when(step >= STEPS[0])
    def second():
        later = step - STEPS[0]
        sum_images(
            1, later, STEPS[1], meta_rest, pixels_rest, normal_ref, sums_ref, plain_ref, work[4:]
        )

    @pl.when(step == STEPS[0] + STEPS[1] - 1)
    def finish():
        slab_reply(me_ref[0], lit_ref, slopes_ref, sums_ref, plain_ref, reply_ref)


def both_sums(me, metas, pixels, around, lit):
    places = (
        lambda s: jnp.minimum(s, STEPS[0] - 1),
        lambda s: jnp.maximum(s - STEPS[0], 0),
    )
    specs, scratch = [pl.BlockSpec(memory_space=pltpu.SMEM)], []
    for part in range(2):
        count, sources, place = PARTS[part][1], SUM_SRC[part], places[part]
        rows = QUARTERS * count + (EXTRA if part == 0 else 0)
        specs.append(pl.BlockSpec((8, sources * count), lambda s, place=place: (0, place(s))))
        specs.append(
            pl.BlockSpec((sources, rows, LANES), lambda s, place=place: (place(s), 0, 0))
        )
        scratch += [pltpu.VMEM((sources * count // 2, 2 * SLAB), BF16)] * 2
        scratch += [pltpu.VMEM((3 * DEVICES, sources * count // 2), BF16)] * 2
    return pl.pallas_call(
        both_kernel,
        grid=(STEPS[0] + STEPS[1],),
        in_specs=specs + [kept((DEVICES, 16, LANES)), kept((DEVICES, SLAB))],
        out_specs=kept((DEVICES, REPLY, LANES)),
        out_shape=jax.ShapeDtypeStruct((DEVICES, REPLY, LANES), BF16),
        scratch_shapes=[
            pltpu.VMEM(shape, dtype) for shape, dtype in (SUMS, PLAIN, NORMALS, SLOPES, ROWS)
        ]
        + scratch,
        compiler_params=pltpu.CompilerParams(vmem_limit_bytes=44 * 1024 * 1024),
    )(me, metas[0], pixels[0], metas[1], pixels[1], around, lit)


def owner_kernel(final, *refs):
    got_ref, surface_ref, hits_ref, height_ref, ends_ref, sides_ref = refs[:6]
    outs, (model_ref, misfit_ref, scalar_ref, mixed_ref) = refs[6:-4], refs[-4:]
    swap, short_swap = swap_matrix(), swap_matrix(16, 8)
    for group in range(DEVICES // 16):
        span = slice(group * 16, group * 16 + 16)
        rows = []
        for matrix, start, count in ((swap, 0, 16), (short_swap, 16, 8)):
            block = got_ref[span, start : start + count, :].reshape(16 * count, LANES)
            turned = jnp.dot(matrix, block, preferred_element_type=F32)
            rows += [turned[j * 16 : j * 16 + 16] for j in range(count)]
        for j in range(10):
            model_ref[j, span] = rows[j]
            misfit_ref[j, span] = rows[10 + j]
        scalar_ref[span] = rows[20]
    scalars = scalar_ref[...]
    cross = scalars[:, 0:1] + scalars[:, 1:2] + scalars[:, 2:3]
    power = scalars[:, 3:4] + scalars[:, 4:5] + scalars[:, 5:6]
    albedo = jnp.sum(cross, keepdims=True) / jnp.sum(power, keepdims=True)
    rest = albedo * (albedo - own_albedo(cross, power))

    def grad(j):
        return jnp.concatenate(
            [albedo * misfit_ref[i] + rest * model_ref[i] for i in (j, j + 1)], axis=1
        )

    row = iota_of((DEVICES, TILE), 0)
    lane = iota_of((DEVICES, TILE), 1)
    along_even, along_odd, halo = grad(4), grad(6), grad(8)
    before = jnp.where(row == 0, pltpu.roll(halo, 1, 0), pltpu.roll(along_odd, 1, 0))
    after = jnp.where(
        row == DEVICES - 1,
        pltpu.roll(halo, DEVICES - 1, 0),
        pltpu.roll(along_even, DEVICES - 1, 0),
    )
    data = (grad(0) + (before - along_odd) * 0.5, grad(2) + (along_even - after) * 0.5)
    old = (surface_ref[:DEVICES], surface_ref[DEVICES:])
    above = jnp.where(row == 0, ends_ref[0:1], pltpu.roll(old[1], 1, 0))
    below = jnp.where(row == DEVICES - 1, ends_ref[1:2], pltpu.roll(old[0], DEVICES - 1, 0))
    vertical = (above + old[1], old[0] + below)
    new = []
    for part in range(2):
        span = slice(part * DEVICES, (part + 1) * DEVICES)
        left = jnp.where(lane == 0, sides_ref[span, 0:1], pltpu.roll(old[part], 1, 1))
        right = jnp.where(
            lane == TILE - 1, sides_ref[span, 1:2], pltpu.roll(old[part], TILE - 1, 1)
        )
        laplace = vertical[part] + left + right - 4.0 * old[part]
        laser = hits_ref[span] * old[part] - height_ref[span]
        new.append(
            old[part]
            - step_size * (data[part] - smooth_weight * laplace + laser_weight * laser)
        )
    if final:
        for part in range(2):
            for half in range(2):
                lanes = slice(half * LANES, half * LANES + LANES)
                mixed_ref[pl.ds(half * TILE + part, DEVICES, 2), :] = new[part][:, lanes]
        for half in range(2):
            outs[0][:, half * LANES : half * LANES + LANES] = mixed_ref[
                half * TILE : half * TILE + TILE
            ]
        return
    outs[0][:DEVICES], outs[0][DEVICES:] = new[0], new[1]
    pieces = around_pieces(new[0], new[1])
    for group in range(DEVICES // 16):
        span = slice(group * 16, group * 16 + 16)
        outs[1][span] = swapped(swap, [item[span] for item in pieces])


def owner_update(final, got, surface, hits, height_sum, rims):
    above, below, left, right = rims
    ends = jnp.concatenate([above, below], axis=0)
    sides = jnp.concatenate([left, right], axis=1)
    out_shape = [jax.ShapeDtypeStruct((TILE, TILE), F32)]
    if not final:
        out_shape.append(jax.ShapeDtypeStruct((DEVICES, 16, LANES), BF16))
    return pl.pallas_call(
        functools.partial(owner_kernel, final),
        out_shape=out_shape,
        scratch_shapes=[
            pltpu.VMEM((10, DEVICES, LANES), F32),
            pltpu.VMEM((10, DEVICES, LANES), F32),
            pltpu.VMEM((DEVICES, LANES), F32),
            pltpu.VMEM((2 * TILE, LANES), F32),
        ],
        compiler_params=pltpu.CompilerParams(vmem_limit_bytes=32 * 1024 * 1024),
    )(got, surface, hits, height_sum, ends, sides)


def shot_sums(slots):
    cell = lax.broadcasted_iota(jnp.int32, (1, TILE), 1).astype(F32)
    present = slots[:, 4:5]
    in_row = jnp.where(slots[:, 0:1] == cell, 1.0, 0.0)
    in_col = jnp.where(slots[:, 1:2] == cell, 1.0, 0.0).astype(BF16)
    left = jnp.concatenate([in_row * slots[:, j : j + 1] * present for j in (4, 2, 3)], axis=1)
    both = lax.dot_general(
        left.astype(BF16), in_col, (((0,), (0,)), ((), ())), preferred_element_type=F32
    )
    return both[:TILE], both[TILE : 2 * TILE] + both[2 * TILE :]


def body(heights, shadow, image_tiles, image_dest, sun_gain, shot_dest, shot_pixel, shot_height):
    me = (lax.axis_index("row") * N_COL + lax.axis_index("col")).astype(jnp.int32)[None]
    packed, surface = pack(
        image_tiles,
        heights,
        shadow,
        image_dest.T,
        sun_gain.T,
        shot_dest.T,
        shot_pixel[None, :],
        shot_height[None, :],
    )
    rims = edges(surface)
    pixels = (exchange(packed), exchange(pack_rest(image_tiles)))
    extra = pixels[0][:, QUARTERS * PARTS[0][1] :, :]
    metas = []
    for start, count in PARTS:
        lists = [
            extra[:, row, at + start : at + start + count]
            for row, at in ((20, 0), (21, 0), (21, IMG), (22, 0), (22, IMG))
        ]
        meta = jnp.stack(lists).astype(F32).reshape(5, DEVICES * count)
        metas.append(jnp.pad(meta, ((0, 3), (0, 0))))
    slab_lit = extra[:, 16:20, :].reshape(DEVICES, SLAB).astype(F32)
    around = extra[:, 0:16, :]
    slots = extra[:, 23, : SHOT_CAP * 5].reshape(DEVICES * SHOT_CAP, 5).astype(F32)
    hits, height_sum = shot_sums(slots)
    begun = first_sums(me, metas[0], pixels[0], around, slab_lit)
    got = exchange(second_sums(me, metas[1], pixels[1], around, slab_lit, *begun))
    surface, around = owner_update(False, got, surface, hits, height_sum, rims)
    around = exchange(around)
    rims = edges(surface)
    got = exchange(both_sums(me, metas, pixels, around, slab_lit))
    return owner_update(True, got, surface, hits, height_sum, rims)[0]


def solution(mesh):
    placed = (
        P("row", "col"),
        P("row", "col"),
        P(("row", "col"), None, None),
        P(("row", "col"), None),
        P(("row", "col"), None),
        P(("row", "col"), None),
        P(("row", "col")),
        P(("row", "col")),
    )
    return jax.shard_map(
        body, mesh=mesh, in_specs=placed, out_specs=P("row", "col"), check_vma=False
    )
```

```python
import functools

import jax
import jax.numpy as jnp
from jax import lax
from jax.experimental import pallas as pl
from jax.experimental.pallas import tpu as pltpu
from jax.sharding import PartitionSpec as P

sharpness = 8.0
step_size = 0.01
smooth_weight = 2.0
laser_weight = 20.0

AXES = ("row", "col")
DEVICES = 128
N_COL = 16
TILE = 256
IMG = 64
SLAB = 512
LANES = 128
QUARTERS = SLAB // LANES
PARTS = ((0, 48), (48, 16))
EXTRA = 24
REPLY = 24
SHOT_CAP = 4
LOG_2 = 0.6931471805599453
F32 = jnp.float32
BF16 = jnp.bfloat16


def exchange(value):
    return lax.all_to_all(value, AXES, split_axis=0, concat_axis=0, tiled=True)


def edges(value):
    out = []
    for axis, dim in (("row", 0), ("col", 1)):
        devices, length = (lax.axis_size(axis), value.shape[dim])
        up = [(i, (i + 1) % devices) for i in range(devices - 1)]
        down = [(j, i) for i, j in up]
        last = lax.slice_in_dim(value, length - 1, length, axis=dim)
        first = lax.slice_in_dim(value, 0, 1, axis=dim)
        out.append(lax.ppermute(last, axis, up))
        out.append(lax.ppermute(first, axis, down))
    return out


def own_albedo(cross, power):
    return jnp.where(power > 0.0, cross / jnp.where(power > 0.0, power, 1.0), 0.0)


PACK_ROWS = 64


def swap_matrix(blocks=16, rows=16):
    to = lax.broadcasted_iota(jnp.int32, (blocks * rows, blocks * rows), 0)
    source = lax.broadcasted_iota(jnp.int32, (blocks * rows, blocks * rows), 1)
    return jnp.where((to % blocks) * rows + to // blocks == source, 1.0, 0.0).astype(BF16)


def iota_of(shape, dim):
    return lax.broadcasted_iota(jnp.int32, shape, dim)


def two_terms(value):
    head = value.astype(BF16)
    return head, (value - head.astype(F32)).astype(BF16)


def swapped(swap, pieces):
    turned = jnp.dot(swap, jnp.concatenate(pieces, axis=0), preferred_element_type=F32)
    return turned.astype(BF16).reshape(16, len(pieces), LANES)


def around_pieces(even, odd):
    four = (pltpu.roll(odd, 1, 0), even, odd, pltpu.roll(even, DEVICES - 1, 0))
    terms = [two_terms(item) for item in four]
    return [
        terms[r][term][:, half * LANES : half * LANES + LANES]
        for term in range(2)
        for r in range(4)
        for half in range(2)
    ]


def shot_rows(target, pixel, height):
    count = target.shape[1]
    head = height.astype(BF16).astype(F32)
    grid_row = jnp.floor(pixel * (1.0 / TILE))
    pair = jnp.floor(grid_row * 0.5)
    columns = jnp.concatenate(
        [
            target,
            (grid_row - 2.0 * pair) * DEVICES + pair,
            pixel - TILE * grid_row,
            head,
            height - head,
            jnp.ones_like(height),
            jnp.zeros((2, count), F32),
        ],
        axis=0,
    ).T
    alike = columns[:, 0:1] == target
    before = iota_of((count, count), 0) < iota_of((count, count), 1)
    rank = jnp.sum(jnp.where(jnp.logical_and(alike, before), 1.0, 0.0), axis=0, keepdims=True)
    lane = iota_of((count, LANES), 1)
    record = jnp.zeros((count, LANES), F32)
    for member in range(5):
        record = jnp.where(lane % 5 == member, columns[:, member + 1 : member + 2], record)
    owned = iota_of((DEVICES, count), 0).astype(F32) == target
    rows = jnp.zeros((DEVICES, LANES), F32)
    for slot in range(SHOT_CAP):
        chosen = jnp.where(jnp.logical_and(owned, rank == slot), 1.0, 0.0).astype(BF16)
        held = jnp.where(lane // 5 == slot, record, 0.0).astype(BF16)
        rows = rows + jnp.dot(chosen, held, preferred_element_type=F32)
    return rows.astype(BF16)


def pack_images(swap, images_ref, out_ref):
    count = images_ref.shape[0]
    for band in range(PACK_ROWS // 16):
        for group in range(count // 16):
            block = images_ref[group * 16 : group * 16 + 16, band * 16 : band * 16 + 16]
            turned = jnp.dot(
                swap, block.reshape(256, TILE), preferred_element_type=F32
            ).astype(BF16)
            for r in range(16):
                for half in range(TILE // LANES):
                    place = ((r % 2) * 2 + half) * count + group * 16
                    out_ref[band * 8 + r // 2, place : place + 16, :] = turned[
                        r * 16 : r * 16 + 16, half * LANES : half * LANES + LANES
                    ]


def pack_rest_kernel(images_ref, out_ref):
    pack_images(swap_matrix(), images_ref, out_ref)


def pack_kernel(
    images_ref, heights_ref, shadow_ref, dest_ref, sun_ref, shot_dest_ref, pixel_ref, shot_height_ref,
    out_ref, split_ref, extra_ref, halves_ref,
):
    step = pl.program_id(0)
    swap = swap_matrix()

    @pl.when(step == 0)
    def start():
        tiles = []
        for source, kind in ((heights_ref, 0), (shadow_ref, 1)):
            parts = []
            for half in range(2):
                lanes = slice(half * LANES, half * LANES + LANES)
                block = source[:, lanes]
                halves_ref[kind * 2 + half] = block if kind == 0 else 1.0 - block.astype(F32)
            for side in range(2):
                parts.append(
                    jnp.concatenate(
                        [halves_ref[kind * 2 + half, pl.ds(side, DEVICES, 2), :] for half in range(2)],
                        axis=1,
                    )
                )
            tiles.append(parts)
        (even, odd), (lit_even, lit_odd) = tiles
        split_ref[:DEVICES] = even
        split_ref[DEVICES:] = odd
        first = around_pieces(even, odd)
        lit = jnp.concatenate([lit_even, lit_odd], axis=1).astype(BF16)
        sun = sun_ref[...].astype(F32)
        dest = dest_ref[...].astype(F32)
        table = [
            jnp.concatenate([dest, jnp.zeros_like(dest)], axis=1),
            jnp.concatenate([sun[0:1], sun[1:2]], axis=1),
            jnp.concatenate([sun[2:3], sun[3:4]], axis=1),
        ]
        second = [lit[:, j * LANES : j * LANES + LANES] for j in range(4)]
        second += [jnp.broadcast_to(item, (DEVICES, LANES)).astype(BF16) for item in table]
        shots = (shot_dest_ref[...].astype(F32), pixel_ref[...].astype(F32), shot_height_ref[...])
        second += [shot_rows(*shots)] + [jnp.zeros((DEVICES, LANES), BF16)] * 8
        for group in range(DEVICES // 16):
            span = slice(group * 16, group * 16 + 16)
            extra_ref[span, 0:16] = swapped(swap, [item[span] for item in first])
            extra_ref[span, 16:32] = swapped(swap, [item[span] for item in second])

    pack_images(swap, images_ref, out_ref)
    per_step = PACK_ROWS // 2
    here = pl.ds(pl.multiple_of(step * per_step, per_step), per_step)
    pixel_rows = QUARTERS * images_ref.shape[0]
    out_ref[:, pixel_rows : pixel_rows + EXTRA, :] = extra_ref[here, 0:EXTRA, :]


def pack(images, heights, shadow, *small):
    per_step = PACK_ROWS // 2
    count = PARTS[0][1]
    rows = QUARTERS * count + EXTRA
    whole = lambda s: (0, 0)
    return pl.pallas_call(
        pack_kernel,
        grid=(DEVICES // per_step,),
        in_specs=[
            pl.BlockSpec((count, PACK_ROWS, TILE), lambda s: (0, s, 0)),
            pl.BlockSpec((TILE, TILE), whole),
            pl.BlockSpec((TILE, TILE), whole),
        ]
        + [pl.BlockSpec(item.shape, whole) for item in small],
        out_specs=[
            pl.BlockSpec((per_step, rows, LANES), lambda s: (s, 0, 0)),
            pl.BlockSpec((TILE, TILE), whole),
        ],
        out_shape=[
            jax.ShapeDtypeStruct((DEVICES, rows, LANES), BF16),
            jax.ShapeDtypeStruct((TILE, TILE), F32),
        ],
        scratch_shapes=[
            pltpu.VMEM((DEVICES, 32, LANES), BF16),
            pltpu.VMEM((4, TILE, LANES), F32),
        ],
        compiler_params=pltpu.CompilerParams(vmem_limit_bytes=58 * 1024 * 1024),
    )(images, heights, shadow, *small)


def pack_rest(images):
    per_step = PACK_ROWS // 2
    start, count = PARTS[1]
    rows = QUARTERS * count
    return pl.pallas_call(
        pack_rest_kernel,
        grid=(DEVICES // per_step,),
        in_specs=[pl.BlockSpec((count, PACK_ROWS, TILE), lambda s: (start // count, s, 0))],
        out_specs=pl.BlockSpec((per_step, rows, LANES), lambda s: (s, 0, 0)),
        out_shape=jax.ShapeDtypeStruct((DEVICES, rows, LANES), BF16),
        compiler_params=pltpu.CompilerParams(vmem_limit_bytes=58 * 1024 * 1024),
        cost_estimate=pl.CostEstimate(
            flops=2 * 256 * TILE * TILE * count, bytes_accessed=4 * TILE * TILE * count, transcendentals=0
        ),
    )(images)


SUM_SRC = (32, 64)
STEPS = (DEVICES // 32, DEVICES // 64)
WIDTH = 2 * SLAB + TILE


def sideways(value):
    lane = iota_of(value.shape, 1)
    column = iota_of(value.shape, 0) % N_COL
    before = pltpu.roll(value, 1, 1)
    first = jnp.where(column == 0, 0.0, pltpu.roll(before, 1, 0))
    after = pltpu.roll(value, TILE - 1, 1)
    last = jnp.where(column == N_COL - 1, 0.0, pltpu.roll(after, DEVICES - 1, 0))
    return jnp.where(lane == 0, first, before), jnp.where(lane == TILE - 1, last, after)


def central_x(value):
    before, after = sideways(value)
    return after - before


def shift_tiles(value, count):
    pad = jnp.zeros((abs(count),) + value.shape[1:], value.dtype)
    if count > 0:
        return jnp.concatenate([pad, value[:-count]], axis=0)
    return jnp.concatenate([value[-count:], pad], axis=0)


def slab_normals(me, around_ref, lit_ref, normal_ref, slopes_ref, rows_ref):
    swap = swap_matrix()
    for group in range(DEVICES // 16):
        span = slice(group * 16, group * 16 + 16)
        turned = jnp.dot(
            swap, around_ref[span].reshape(256, LANES), preferred_element_type=F32
        )
        fine = turned[:128] + turned[128:]
        for r in range(4):
            for half in range(2):
                at = (2 * r + half) * 16
                rows_ref[r, span, half * LANES : half * LANES + LANES] = fine[at : at + 16]
    rows = [rows_ref[r] for r in range(4)]
    top = jnp.where(me == 0, shift_tiles(rows[0], N_COL), rows[0])
    bottom = jnp.where(me == DEVICES - 1, shift_tiles(rows[3], -N_COL), rows[3])
    slope_x = jnp.concatenate([central_x(rows[1]), central_x(rows[2])], axis=1) * 0.5
    slope_y = jnp.concatenate([rows[2] - top, bottom - rows[1]], axis=1) * 0.5
    inverse = lax.rsqrt(1.0 + slope_x * slope_x + slope_y * slope_y)
    slopes_ref[0], slopes_ref[1], slopes_ref[2] = slope_x, slope_y, inverse
    scale = 0.5 * sharpness
    x_head, x_tail = two_terms(-slope_x * inverse * scale)
    y_head, y_tail = two_terms(-slope_y * inverse * scale)
    steep = ((inverse - 1.0) * scale).astype(BF16)
    flat = jnp.where(lit_ref[...] > 0.5, scale, -2048.0).astype(BF16)
    for place, item in enumerate((x_head, y_head, x_tail, y_tail, steep, flat)):
        normal_ref[place * DEVICES : (place + 1) * DEVICES] = item


def slab_reply(me, lit_ref, slopes_ref, sums_ref, plain_ref, reply_ref):
    lit = lit_ref[...]
    slope_x, slope_y, inverse = slopes_ref[0], slopes_ref[1], slopes_ref[2]
    cube = inverse * inverse * inverse
    lane = iota_of((16, LANES), 1)
    scalars = jnp.zeros((16, LANES), BF16)
    totals = []
    for part in range(2):
        value = jnp.sum(plain_ref[:, part * SLAB : (part + 1) * SLAB], keepdims=True)
        total = jnp.zeros((1, 1), F32)
        for term in range(3):
            head = value.astype(BF16).astype(F32)
            scalars = jnp.where(lane == part * 3 + term, head, scalars.astype(F32)).astype(BF16)
            value = value - head
            total = total + head
        totals.append(total)
    guess = own_albedo(totals[0], totals[1])
    fields = []
    for part in range(2):
        by_x, by_y, by_z = (
            sums_ref[j * DEVICES : (j + 1) * DEVICES, part * SLAB : (part + 1) * SLAB]
            for j in range(3)
        )
        turned = (by_z - slope_x * by_x - slope_y * by_y) * cube
        grad_x = -lit * (by_x * inverse + slope_x * turned)
        grad_y = -lit * (by_y * inverse + slope_y * turned)
        across = jnp.concatenate([central_x(grad_x[:, :TILE]), central_x(grad_x[:, TILE:])], axis=1)
        halo = jnp.where(
            me == 0, shift_tiles(grad_y[:, :TILE], -N_COL), shift_tiles(grad_y[:, TILE:], N_COL)
        )
        fields.append(jnp.concatenate([across * (-0.5), grad_y, halo], axis=1))
    seen, model = fields
    flat = jnp.concatenate([model.astype(BF16), (guess * model - seen).astype(BF16)], axis=1)
    swap, short_swap = swap_matrix(), swap_matrix(8, 16)
    for group in range(DEVICES // 16):
        span = slice(group * 16, group * 16 + 16)
        pieces = [flat[span, j * LANES : (j + 1) * LANES] for j in range(20)]
        pieces = pieces + [scalars] + [jnp.zeros((16, LANES), BF16)] * 3
        reply_ref[span, 0:16, :] = swapped(swap, pieces[:16])
        reply_ref[span, 16:24, :] = swapped(short_swap, pieces[16:])


def sum_images(part, step, steps, meta_ref, pixels_ref, normal_ref, sums_ref, plain_ref, work):
    first_w, second_w, first_p, second_p = work
    count = PARTS[part][1]
    half_src = SUM_SRC[part] // 2
    half_img = half_src * count

    def front(side, w_ref, p_ref):
        meta = meta_ref[:, side * half_img : (side + 1) * half_img]
        cols = meta.T
        hot = iota_of((half_img, DEVICES), 1).astype(F32) == cols[:, 0:1]
        sun = [jnp.where(hot, cols[:, j : j + 1], 0.0).astype(BF16) for j in (1, 2, 3)]
        pick = jnp.concatenate([sun[0], sun[1], sun[0], sun[1], sun[2], sun[2]], axis=1)
        hot_t = iota_of((DEVICES, half_img), 0).astype(F32) == meta[0:1, :]
        for j in range(3):
            p_ref[j * DEVICES : (j + 1) * DEVICES] = jnp.where(
                hot_t, meta[j + 1 : j + 2, :], 0.0
            ).astype(BF16)
        chunks = half_img // (192 if count == 48 else 128)
        few, images = (half_src // chunks, half_img // chunks)
        for chunk in range(chunks):
            span = slice(chunk * images, (chunk + 1) * images)
            src = slice(side * half_src + chunk * few, side * half_src + (chunk + 1) * few)
            half_angle = jnp.dot(pick[span], normal_ref[...], preferred_element_type=F32)
            gain = cols[span, 4:5]
            bend = jnp.tanh(half_angle)
            refl = (jnp.log2(1.0 - bend) - 1.0) * (gain * (-LOG_2 / sharpness))
            sigma = bend * (gain * 0.5) + gain * 0.5
            seen = jnp.concatenate(
                [
                    pixels_ref[src, q * count : q * count + count, :].reshape(images, LANES)
                    for q in range(QUARTERS)
                ],
                axis=1,
            ).astype(F32)
            w_ref[span, :SLAB] = (seen * sigma).astype(BF16)
            w_ref[span, SLAB:] = (refl * sigma).astype(BF16)
            plain_ref[:, :SLAB] += jnp.sum((seen * refl).reshape(-1, 8, SLAB), axis=0)
            plain_ref[:, SLAB:] += jnp.sum((refl * refl).reshape(-1, 8, SLAB), axis=0)

    def back(w_ref, p_ref):
        sums_ref[...] += jnp.dot(p_ref[...], w_ref[...], preferred_element_type=F32)

    @pl.when(step == 0)
    def start():
        second_w[...] = jnp.zeros_like(second_w)
        second_p[...] = jnp.zeros_like(second_p)

    back(second_w, second_p)
    front(0, first_w, first_p)
    back(first_w, first_p)
    front(1, second_w, second_p)

    @pl.when(step == steps - 1)
    def finish():
        back(second_w, second_p)


def first_kernel(
    me_ref, meta_ref, pixels_ref, around_ref, lit_ref,
    sums_ref, plain_ref, normal_ref, slopes_ref, rows_ref, *work,
):
    @pl.when(pl.program_id(0) == 0)
    def start():
        sums_ref[...] = jnp.zeros_like(sums_ref)
        plain_ref[...] = jnp.zeros_like(plain_ref)
        slab_normals(me_ref[0], around_ref, lit_ref, normal_ref, slopes_ref, rows_ref)

    sum_images(
        0, pl.program_id(0), STEPS[0], meta_ref, pixels_ref, normal_ref, sums_ref, plain_ref, work
    )


def second_kernel(
    me_ref, meta_ref, pixels_ref, around_ref, lit_ref, sums_in, plain_in,
    reply_ref, sums_ref, plain_ref, normal_ref, slopes_ref, rows_ref, *work,
):
    @pl.when(pl.program_id(0) == 0)
    def start():
        sums_ref[...] = sums_in[...]
        plain_ref[...] = plain_in[...]
        slab_normals(me_ref[0], around_ref, lit_ref, normal_ref, slopes_ref, rows_ref)

    sum_images(
        1, pl.program_id(0), STEPS[1], meta_ref, pixels_ref, normal_ref, sums_ref, plain_ref, work
    )

    @pl.when(pl.program_id(0) == pl.num_programs(0) - 1)
    def finish():
        slab_reply(me_ref[0], lit_ref, slopes_ref, sums_ref, plain_ref, reply_ref)


SUMS = ((3 * DEVICES, 2 * SLAB), F32)
PLAIN = ((8, 2 * SLAB), F32)
NORMALS = ((6 * DEVICES, SLAB), BF16)
SLOPES = ((3, DEVICES, SLAB), F32)
ROWS = ((4, DEVICES, TILE), F32)


def kept(shape):
    return pl.BlockSpec(shape, lambda s: (0,) * len(shape))


def sum_call(part, kernel, inputs, specs, outs, scratch):
    count, sources = PARTS[part][1], SUM_SRC[part]
    half = sources * count // 2
    rows = QUARTERS * count + (EXTRA if part == 0 else 0)
    cells = DEVICES * count * SLAB
    return pl.pallas_call(
        kernel,
        grid=(DEVICES // sources,),
        in_specs=[
            pl.BlockSpec(memory_space=pltpu.SMEM),
            pl.BlockSpec((8, sources * count), lambda s: (0, s)),
            pl.BlockSpec((sources, rows, LANES), lambda s: (s, 0, 0)),
        ]
        + specs,
        out_specs=[kept(shape) for shape, dtype in outs],
        out_shape=[jax.ShapeDtypeStruct(shape, dtype) for shape, dtype in outs],
        scratch_shapes=[pltpu.VMEM(shape, dtype) for shape, dtype in scratch]
        + [pltpu.VMEM((half, 2 * SLAB), BF16)] * 2
        + [pltpu.VMEM((3 * DEVICES, half), BF16)] * 2,
        compiler_params=pltpu.CompilerParams(vmem_limit_bytes=44 * 1024 * 1024),
        cost_estimate=pl.CostEstimate(
            flops=2 * 12 * DEVICES * cells, bytes_accessed=4 * cells, transcendentals=2 * cells
        ),
    )(*inputs)


def first_sums(me, meta, pixels, around, lit):
    return sum_call(
        0,
        first_kernel,
        (me, meta, pixels, around, lit),
        [kept((DEVICES, 16, LANES)), kept((DEVICES, SLAB))],
        (SUMS, PLAIN),
        (NORMALS, SLOPES, ROWS),
    )


def second_sums(me, meta, pixels, around, lit, sums, plain):
    return sum_call(
        1,
        second_kernel,
        (me, meta, pixels, around, lit, sums, plain),
        [kept((DEVICES, 16, LANES)), kept((DEVICES, SLAB)), kept(SUMS[0]), kept(PLAIN[0])],
        (((DEVICES, REPLY, LANES), BF16),),
        (SUMS, PLAIN, NORMALS, SLOPES, ROWS),
    )[0]


def both_kernel(
    me_ref, meta_ref, pixels_ref, meta_rest, pixels_rest, around_ref, lit_ref,
    reply_ref, sums_ref, plain_ref, normal_ref, slopes_ref, rows_ref, *work,
):
    step = pl.program_id(0)

    @pl.when(step == 0)
    def start():
        sums_ref[...] = jnp.zeros_like(sums_ref)
        plain_ref[...] = jnp.zeros_like(plain_ref)
        slab_normals(me_ref[0], around_ref, lit_ref, normal_ref, slopes_ref, rows_ref)

    @pl.when(step < STEPS[0])
    def first():
        sum_images(
            0, step, STEPS[0], meta_ref, pixels_ref, normal_ref, sums_ref, plain_ref, work[:4]
        )

    @pl.when(step >= STEPS[0])
    def second():
        later = step - STEPS[0]
        sum_images(
            1, later, STEPS[1], meta_rest, pixels_rest, normal_ref, sums_ref, plain_ref, work[4:]
        )

    @pl.when(step == STEPS[0] + STEPS[1] - 1)
    def finish():
        slab_reply(me_ref[0], lit_ref, slopes_ref, sums_ref, plain_ref, reply_ref)


def both_sums(me, metas, pixels, around, lit):
    places = (
        lambda s: jnp.minimum(s, STEPS[0] - 1),
        lambda s: jnp.maximum(s - STEPS[0], 0),
    )
    specs, scratch = [pl.BlockSpec(memory_space=pltpu.SMEM)], []
    for part in range(2):
        count, sources, place = PARTS[part][1], SUM_SRC[part], places[part]
        rows = QUARTERS * count + (EXTRA if part == 0 else 0)
        specs.append(pl.BlockSpec((8, sources * count), lambda s, place=place: (0, place(s))))
        specs.append(
            pl.BlockSpec((sources, rows, LANES), lambda s, place=place: (place(s), 0, 0))
        )
        scratch += [pltpu.VMEM((sources * count // 2, 2 * SLAB), BF16)] * 2
        scratch += [pltpu.VMEM((3 * DEVICES, sources * count // 2), BF16)] * 2
    return pl.pallas_call(
        both_kernel,
        grid=(STEPS[0] + STEPS[1],),
        in_specs=specs + [kept((DEVICES, 16, LANES)), kept((DEVICES, SLAB))],
        out_specs=kept((DEVICES, REPLY, LANES)),
        out_shape=jax.ShapeDtypeStruct((DEVICES, REPLY, LANES), BF16),
        scratch_shapes=[
            pltpu.VMEM(shape, dtype) for shape, dtype in (SUMS, PLAIN, NORMALS, SLOPES, ROWS)
        ]
        + scratch,
        compiler_params=pltpu.CompilerParams(vmem_limit_bytes=44 * 1024 * 1024),
    )(me, metas[0], pixels[0], metas[1], pixels[1], around, lit)


def owner_kernel(final, *refs):
    got_ref, surface_ref, hits_ref, height_ref, ends_ref, sides_ref = refs[:6]
    outs, (model_ref, misfit_ref, scalar_ref, mixed_ref) = refs[6:-4], refs[-4:]
    swap, short_swap = swap_matrix(), swap_matrix(16, 8)
    for group in range(DEVICES // 16):
        span = slice(group * 16, group * 16 + 16)
        rows = []
        for matrix, start, count in ((swap, 0, 16), (short_swap, 16, 8)):
            block = got_ref[span, start : start + count, :].reshape(16 * count, LANES)
            turned = jnp.dot(matrix, block, preferred_element_type=F32)
            rows += [turned[j * 16 : j * 16 + 16] for j in range(count)]
        for j in range(10):
            model_ref[j, span] = rows[j]
            misfit_ref[j, span] = rows[10 + j]
        scalar_ref[span] = rows[20]
    scalars = scalar_ref[...]
    cross = scalars[:, 0:1] + scalars[:, 1:2] + scalars[:, 2:3]
    power = scalars[:, 3:4] + scalars[:, 4:5] + scalars[:, 5:6]
    albedo = jnp.sum(cross, keepdims=True) / jnp.sum(power, keepdims=True)
    rest = albedo * (albedo - own_albedo(cross, power))

    def grad(j):
        return jnp.concatenate(
            [albedo * misfit_ref[i] + rest * model_ref[i] for i in (j, j + 1)], axis=1
        )

    row = iota_of((DEVICES, TILE), 0)
    lane = iota_of((DEVICES, TILE), 1)
    along_even, along_odd, halo = grad(4), grad(6), grad(8)
    before = jnp.where(row == 0, pltpu.roll(halo, 1, 0), pltpu.roll(along_odd, 1, 0))
    after = jnp.where(
        row == DEVICES - 1,
        pltpu.roll(halo, DEVICES - 1, 0),
        pltpu.roll(along_even, DEVICES - 1, 0),
    )
    data = (grad(0) + (before - along_odd) * 0.5, grad(2) + (along_even - after) * 0.5)
    old = (surface_ref[:DEVICES], surface_ref[DEVICES:])
    above = jnp.where(row == 0, ends_ref[0:1], pltpu.roll(old[1], 1, 0))
    below = jnp.where(row == DEVICES - 1, ends_ref[1:2], pltpu.roll(old[0], DEVICES - 1, 0))
    vertical = (above + old[1], old[0] + below)
    new = []
    for part in range(2):
        span = slice(part * DEVICES, (part + 1) * DEVICES)
        left = jnp.where(lane == 0, sides_ref[span, 0:1], pltpu.roll(old[part], 1, 1))
        right = jnp.where(
            lane == TILE - 1, sides_ref[span, 1:2], pltpu.roll(old[part], TILE - 1, 1)
        )
        laplace = vertical[part] + left + right - 4.0 * old[part]
        laser = hits_ref[span] * old[part] - height_ref[span]
        new.append(
            old[part]
            - step_size * (data[part] - smooth_weight * laplace + laser_weight * laser)
        )
    if final:
        for part in range(2):
            for half in range(2):
                lanes = slice(half * LANES, half * LANES + LANES)
                mixed_ref[pl.ds(half * TILE + part, DEVICES, 2), :] = new[part][:, lanes]
        for half in range(2):
            outs[0][:, half * LANES : half * LANES + LANES] = mixed_ref[
                half * TILE : half * TILE + TILE
            ]
        return
    outs[0][:DEVICES], outs[0][DEVICES:] = new[0], new[1]
    pieces = around_pieces(new[0], new[1])
    for group in range(DEVICES // 16):
        span = slice(group * 16, group * 16 + 16)
        outs[1][span] = swapped(swap, [item[span] for item in pieces])


def owner_update(final, got, surface, hits, height_sum, rims):
    above, below, left, right = rims
    ends = jnp.concatenate([above, below], axis=0)
    sides = jnp.concatenate([left, right], axis=1)
    out_shape = [jax.ShapeDtypeStruct((TILE, TILE), F32)]
    if not final:
        out_shape.append(jax.ShapeDtypeStruct((DEVICES, 16, LANES), BF16))
    return pl.pallas_call(
        functools.partial(owner_kernel, final),
        out_shape=out_shape,
        scratch_shapes=[
            pltpu.VMEM((10, DEVICES, LANES), F32),
            pltpu.VMEM((10, DEVICES, LANES), F32),
            pltpu.VMEM((DEVICES, LANES), F32),
            pltpu.VMEM((2 * TILE, LANES), F32),
        ],
        compiler_params=pltpu.CompilerParams(vmem_limit_bytes=32 * 1024 * 1024),
    )(got, surface, hits, height_sum, ends, sides)


def shot_sums(slots):
    cell = lax.broadcasted_iota(jnp.int32, (1, TILE), 1).astype(F32)
    present = slots[:, 4:5]
    in_row = jnp.where(slots[:, 0:1] == cell, 1.0, 0.0)
    in_col = jnp.where(slots[:, 1:2] == cell, 1.0, 0.0).astype(BF16)
    left = jnp.concatenate([in_row * slots[:, j : j + 1] * present for j in (4, 2, 3)], axis=1)
    both = lax.dot_general(
        left.astype(BF16), in_col, (((0,), (0,)), ((), ())), preferred_element_type=F32
    )
    return both[:TILE], both[TILE : 2 * TILE] + both[2 * TILE :]


def body(heights, shadow, image_tiles, image_dest, sun_gain, shot_dest, shot_pixel, shot_height):
    me = (lax.axis_index("row") * N_COL + lax.axis_index("col")).astype(jnp.int32)[None]
    packed, surface = pack(
        image_tiles,
        heights,
        shadow,
        image_dest.T,
        sun_gain.T,
        shot_dest.T,
        shot_pixel[None, :],
        shot_height[None, :],
    )
    rims = edges(surface)
    pixels = (exchange(packed), exchange(pack_rest(image_tiles)))
    extra = pixels[0][:, QUARTERS * PARTS[0][1] :, :]
    metas = []
    for start, count in PARTS:
        lists = [
            extra[:, row, at + start : at + start + count]
            for row, at in ((20, 0), (21, 0), (21, IMG), (22, 0), (22, IMG))
        ]
        meta = jnp.stack(lists).astype(F32).reshape(5, DEVICES * count)
        metas.append(jnp.pad(meta, ((0, 3), (0, 0))))
    slab_lit = extra[:, 16:20, :].reshape(DEVICES, SLAB).astype(F32)
    around = extra[:, 0:16, :]
    slots = extra[:, 23, : SHOT_CAP * 5].reshape(DEVICES * SHOT_CAP, 5).astype(F32)
    hits, height_sum = shot_sums(slots)
    begun = first_sums(me, metas[0], pixels[0], around, slab_lit)
    got = exchange(second_sums(me, metas[1], pixels[1], around, slab_lit, *begun))
    surface, around = owner_update(False, got, surface, hits, height_sum, rims)
    around = exchange(around)
    rims = edges(surface)
    around, above, below = lax.optimization_barrier((around, rims[0], rims[1]))
    rims = [above, below] + rims[2:]
    got = exchange(both_sums(me, metas, pixels, around, slab_lit))
    return owner_update(True, got, surface, hits, height_sum, rims)[0]


def solution(mesh):
    placed = (
        P("row", "col"),
        P("row", "col"),
        P(("row", "col"), None, None),
        P(("row", "col"), None),
        P(("row", "col"), None),
        P(("row", "col"), None),
        P(("row", "col")),
        P(("row", "col")),
    )
    return jax.shard_map(
        body, mesh=mesh, in_specs=placed, out_specs=P("row", "col"), check_vma=False
    )
```

```python
import functools

import jax
import jax.numpy as jnp
from jax import lax
from jax.experimental import pallas as pl
from jax.experimental.pallas import tpu as pltpu
from jax.sharding import PartitionSpec as P

sharpness = 8.0
step_size = 0.01
smooth_weight = 2.0
laser_weight = 20.0

AXES = ("row", "col")
DEVICES = 128
N_COL = 16
TILE = 256
IMG = 64
SLAB = 512
LANES = 128
QUARTERS = SLAB // LANES
PARTS = ((0, 48), (48, 16))
EXTRA = 24
REPLY = 24
SHOT_CAP = 4
LOG_2 = 0.6931471805599453
F32 = jnp.float32
BF16 = jnp.bfloat16


def exchange(value):
    return lax.all_to_all(value, AXES, split_axis=0, concat_axis=0, tiled=True)


def edges(value):
    out = []
    for axis, dim in (("row", 0), ("col", 1)):
        devices, length = (lax.axis_size(axis), value.shape[dim])
        up = [(i, (i + 1) % devices) for i in range(devices - 1)]
        down = [(j, i) for i, j in up]
        last = lax.slice_in_dim(value, length - 1, length, axis=dim)
        first = lax.slice_in_dim(value, 0, 1, axis=dim)
        out.append(lax.ppermute(last, axis, up))
        out.append(lax.ppermute(first, axis, down))
    return out


def own_albedo(cross, power):
    return jnp.where(power > 0.0, cross / jnp.where(power > 0.0, power, 1.0), 0.0)


PACK_ROWS = 64


def swap_matrix(blocks=16, rows=16):
    to = lax.broadcasted_iota(jnp.int32, (blocks * rows, blocks * rows), 0)
    source = lax.broadcasted_iota(jnp.int32, (blocks * rows, blocks * rows), 1)
    return jnp.where((to % blocks) * rows + to // blocks == source, 1.0, 0.0).astype(BF16)


def iota_of(shape, dim):
    return lax.broadcasted_iota(jnp.int32, shape, dim)


def two_terms(value):
    head = value.astype(BF16)
    return head, (value - head.astype(F32)).astype(BF16)


def swapped(swap, pieces):
    turned = jnp.dot(swap, jnp.concatenate(pieces, axis=0), preferred_element_type=F32)
    return turned.astype(BF16).reshape(16, len(pieces), LANES)


def around_pieces(even, odd):
    four = (pltpu.roll(odd, 1, 0), even, odd, pltpu.roll(even, DEVICES - 1, 0))
    terms = [two_terms(item) for item in four]
    return [
        terms[r][term][:, half * LANES : half * LANES + LANES]
        for term in range(2)
        for r in range(4)
        for half in range(2)
    ]


def shot_rows(target, pixel, height):
    count = target.shape[1]
    head = height.astype(BF16).astype(F32)
    grid_row = jnp.floor(pixel * (1.0 / TILE))
    pair = jnp.floor(grid_row * 0.5)
    columns = jnp.concatenate(
        [
            target,
            (grid_row - 2.0 * pair) * DEVICES + pair,
            pixel - TILE * grid_row,
            head,
            height - head,
            jnp.ones_like(height),
            jnp.zeros((2, count), F32),
        ],
        axis=0,
    ).T
    alike = columns[:, 0:1] == target
    before = iota_of((count, count), 0) < iota_of((count, count), 1)
    rank = jnp.sum(jnp.where(jnp.logical_and(alike, before), 1.0, 0.0), axis=0, keepdims=True)
    lane = iota_of((count, LANES), 1)
    record = jnp.zeros((count, LANES), F32)
    for member in range(5):
        record = jnp.where(lane % 5 == member, columns[:, member + 1 : member + 2], record)
    owned = iota_of((DEVICES, count), 0).astype(F32) == target
    rows = jnp.zeros((DEVICES, LANES), F32)
    for slot in range(SHOT_CAP):
        chosen = jnp.where(jnp.logical_and(owned, rank == slot), 1.0, 0.0).astype(BF16)
        held = jnp.where(lane // 5 == slot, record, 0.0).astype(BF16)
        rows = rows + jnp.dot(chosen, held, preferred_element_type=F32)
    return rows.astype(BF16)


def pack_images(swap, images_ref, out_ref):
    count = images_ref.shape[0]
    for band in range(PACK_ROWS // 16):
        for group in range(count // 16):
            block = images_ref[group * 16 : group * 16 + 16, band * 16 : band * 16 + 16]
            turned = jnp.dot(
                swap, block.reshape(256, TILE), preferred_element_type=F32
            ).astype(BF16)
            for r in range(16):
                for half in range(TILE // LANES):
                    place = ((r % 2) * 2 + half) * count + group * 16
                    out_ref[band * 8 + r // 2, place : place + 16, :] = turned[
                        r * 16 : r * 16 + 16, half * LANES : half * LANES + LANES
                    ]


def pack_rest_kernel(images_ref, out_ref):
    pack_images(swap_matrix(), images_ref, out_ref)


def pack_kernel(
    images_ref, heights_ref, shadow_ref, dest_ref, sun_ref, shot_dest_ref, pixel_ref, shot_height_ref,
    out_ref, split_ref, extra_ref, halves_ref,
):
    step = pl.program_id(0)
    swap = swap_matrix()

    @pl.when(step == 0)
    def start():
        tiles = []
        for source, kind in ((heights_ref, 0), (shadow_ref, 1)):
            parts = []
            for half in range(2):
                lanes = slice(half * LANES, half * LANES + LANES)
                block = source[:, lanes]
                halves_ref[kind * 2 + half] = block if kind == 0 else 1.0 - block.astype(F32)
            for side in range(2):
                parts.append(
                    jnp.concatenate(
                        [halves_ref[kind * 2 + half, pl.ds(side, DEVICES, 2), :] for half in range(2)],
                        axis=1,
                    )
                )
            tiles.append(parts)
        (even, odd), (lit_even, lit_odd) = tiles
        split_ref[:DEVICES] = even
        split_ref[DEVICES:] = odd
        first = around_pieces(even, odd)
        lit = jnp.concatenate([lit_even, lit_odd], axis=1).astype(BF16)
        sun = sun_ref[...].astype(F32)
        dest = dest_ref[...].astype(F32)
        table = [
            jnp.concatenate([dest, jnp.zeros_like(dest)], axis=1),
            jnp.concatenate([sun[0:1], sun[1:2]], axis=1),
            jnp.concatenate([sun[2:3], sun[3:4]], axis=1),
        ]
        second = [lit[:, j * LANES : j * LANES + LANES] for j in range(4)]
        second += [jnp.broadcast_to(item, (DEVICES, LANES)).astype(BF16) for item in table]
        shots = (shot_dest_ref[...].astype(F32), pixel_ref[...].astype(F32), shot_height_ref[...])
        second += [shot_rows(*shots)] + [jnp.zeros((DEVICES, LANES), BF16)] * 8
        for group in range(DEVICES // 16):
            span = slice(group * 16, group * 16 + 16)
            extra_ref[span, 0:16] = swapped(swap, [item[span] for item in first])
            extra_ref[span, 16:32] = swapped(swap, [item[span] for item in second])

    pack_images(swap, images_ref, out_ref)
    per_step = PACK_ROWS // 2
    here = pl.ds(pl.multiple_of(step * per_step, per_step), per_step)
    pixel_rows = QUARTERS * images_ref.shape[0]
    out_ref[:, pixel_rows : pixel_rows + EXTRA, :] = extra_ref[here, 0:EXTRA, :]


def pack(images, heights, shadow, *small):
    per_step = PACK_ROWS // 2
    count = PARTS[0][1]
    rows = QUARTERS * count + EXTRA
    whole = lambda s: (0, 0)
    return pl.pallas_call(
        pack_kernel,
        grid=(DEVICES // per_step,),
        in_specs=[
            pl.BlockSpec((count, PACK_ROWS, TILE), lambda s: (0, s, 0)),
            pl.BlockSpec((TILE, TILE), whole),
            pl.BlockSpec((TILE, TILE), whole),
        ]
        + [pl.BlockSpec(item.shape, whole) for item in small],
        out_specs=[
            pl.BlockSpec((per_step, rows, LANES), lambda s: (s, 0, 0)),
            pl.BlockSpec((TILE, TILE), whole),
        ],
        out_shape=[
            jax.ShapeDtypeStruct((DEVICES, rows, LANES), BF16),
            jax.ShapeDtypeStruct((TILE, TILE), F32),
        ],
        scratch_shapes=[
            pltpu.VMEM((DEVICES, 32, LANES), BF16),
            pltpu.VMEM((4, TILE, LANES), F32),
        ],
        compiler_params=pltpu.CompilerParams(vmem_limit_bytes=58 * 1024 * 1024),
    )(images, heights, shadow, *small)


def pack_rest(images):
    per_step = PACK_ROWS // 2
    start, count = PARTS[1]
    rows = QUARTERS * count
    return pl.pallas_call(
        pack_rest_kernel,
        grid=(DEVICES // per_step,),
        in_specs=[pl.BlockSpec((count, PACK_ROWS, TILE), lambda s: (start // count, s, 0))],
        out_specs=pl.BlockSpec((per_step, rows, LANES), lambda s: (s, 0, 0)),
        out_shape=jax.ShapeDtypeStruct((DEVICES, rows, LANES), BF16),
        compiler_params=pltpu.CompilerParams(vmem_limit_bytes=58 * 1024 * 1024),
        cost_estimate=pl.CostEstimate(
            flops=2 * 256 * TILE * TILE * count, bytes_accessed=4 * TILE * TILE * count, transcendentals=0
        ),
    )(images)


SUM_SRC = (32, 64)
STEPS = (DEVICES // 32, DEVICES // 64)
WIDTH = 2 * SLAB + TILE


def sideways(value):
    lane = iota_of(value.shape, 1)
    column = iota_of(value.shape, 0) % N_COL
    before = pltpu.roll(value, 1, 1)
    first = jnp.where(column == 0, 0.0, pltpu.roll(before, 1, 0))
    after = pltpu.roll(value, TILE - 1, 1)
    last = jnp.where(column == N_COL - 1, 0.0, pltpu.roll(after, DEVICES - 1, 0))
    return jnp.where(lane == 0, first, before), jnp.where(lane == TILE - 1, last, after)


def central_x(value):
    before, after = sideways(value)
    return after - before


def shift_tiles(value, count):
    pad = jnp.zeros((abs(count),) + value.shape[1:], value.dtype)
    if count > 0:
        return jnp.concatenate([pad, value[:-count]], axis=0)
    return jnp.concatenate([value[-count:], pad], axis=0)


def slab_normals(me, around_ref, lit_ref, normal_ref, slopes_ref, rows_ref):
    swap = swap_matrix()
    for group in range(DEVICES // 16):
        span = slice(group * 16, group * 16 + 16)
        turned = jnp.dot(
            swap, around_ref[span].reshape(256, LANES), preferred_element_type=F32
        )
        fine = turned[:128] + turned[128:]
        for r in range(4):
            for half in range(2):
                at = (2 * r + half) * 16
                rows_ref[r, span, half * LANES : half * LANES + LANES] = fine[at : at + 16]
    rows = [rows_ref[r] for r in range(4)]
    top = jnp.where(me == 0, shift_tiles(rows[0], N_COL), rows[0])
    bottom = jnp.where(me == DEVICES - 1, shift_tiles(rows[3], -N_COL), rows[3])
    slope_x = jnp.concatenate([central_x(rows[1]), central_x(rows[2])], axis=1) * 0.5
    slope_y = jnp.concatenate([rows[2] - top, bottom - rows[1]], axis=1) * 0.5
    inverse = lax.rsqrt(1.0 + slope_x * slope_x + slope_y * slope_y)
    slopes_ref[0], slopes_ref[1], slopes_ref[2] = slope_x, slope_y, inverse
    scale = 0.5 * sharpness
    x_head, x_tail = two_terms(-slope_x * inverse * scale)
    y_head, y_tail = two_terms(-slope_y * inverse * scale)
    steep = ((inverse - 1.0) * scale).astype(BF16)
    flat = jnp.where(lit_ref[...] > 0.5, scale, -2048.0).astype(BF16)
    for place, item in enumerate((x_head, y_head, x_tail, y_tail, steep, flat)):
        normal_ref[place * DEVICES : (place + 1) * DEVICES] = item


def slab_reply(me, lit_ref, slopes_ref, sums_ref, plain_ref, reply_ref):
    lit = lit_ref[...]
    slope_x, slope_y, inverse = slopes_ref[0], slopes_ref[1], slopes_ref[2]
    cube = inverse * inverse * inverse
    lane = iota_of((16, LANES), 1)
    scalars = jnp.zeros((16, LANES), BF16)
    totals = []
    for part in range(2):
        value = jnp.sum(plain_ref[:, part * SLAB : (part + 1) * SLAB], keepdims=True)
        total = jnp.zeros((1, 1), F32)
        for term in range(3):
            head = value.astype(BF16).astype(F32)
            scalars = jnp.where(lane == part * 3 + term, head, scalars.astype(F32)).astype(BF16)
            value = value - head
            total = total + head
        totals.append(total)
    guess = own_albedo(totals[0], totals[1])
    fields = []
    for part in range(2):
        by_x, by_y, by_z = (
            sums_ref[j * DEVICES : (j + 1) * DEVICES, part * SLAB : (part + 1) * SLAB]
            for j in range(3)
        )
        turned = (by_z - slope_x * by_x - slope_y * by_y) * cube
        grad_x = -lit * (by_x * inverse + slope_x * turned)
        grad_y = -lit * (by_y * inverse + slope_y * turned)
        across = jnp.concatenate([central_x(grad_x[:, :TILE]), central_x(grad_x[:, TILE:])], axis=1)
        halo = jnp.where(
            me == 0, shift_tiles(grad_y[:, :TILE], -N_COL), shift_tiles(grad_y[:, TILE:], N_COL)
        )
        fields.append(jnp.concatenate([across * (-0.5), grad_y, halo], axis=1))
    seen, model = fields
    flat = jnp.concatenate([model.astype(BF16), (guess * model - seen).astype(BF16)], axis=1)
    swap, short_swap = swap_matrix(), swap_matrix(8, 16)
    for group in range(DEVICES // 16):
        span = slice(group * 16, group * 16 + 16)
        pieces = [flat[span, j * LANES : (j + 1) * LANES] for j in range(20)]
        pieces = pieces + [scalars] + [jnp.zeros((16, LANES), BF16)] * 3
        reply_ref[span, 0:16, :] = swapped(swap, pieces[:16])
        reply_ref[span, 16:24, :] = swapped(short_swap, pieces[16:])


def sum_images(part, step, steps, meta_ref, pixels_ref, normal_ref, sums_ref, plain_ref, work):
    first_w, second_w, first_p, second_p = work
    count = PARTS[part][1]
    half_src = SUM_SRC[part] // 2
    half_img = half_src * count

    def front(side, w_ref, p_ref):
        meta = meta_ref[:, side * half_img : (side + 1) * half_img]
        cols = meta.T
        hot = iota_of((half_img, DEVICES), 1).astype(F32) == cols[:, 0:1]
        sun = [jnp.where(hot, cols[:, j : j + 1], 0.0).astype(BF16) for j in (1, 2, 3)]
        pick = jnp.concatenate([sun[0], sun[1], sun[0], sun[1], sun[2], sun[2]], axis=1)
        hot_t = iota_of((DEVICES, half_img), 0).astype(F32) == meta[0:1, :]
        for j in range(3):
            p_ref[j * DEVICES : (j + 1) * DEVICES] = jnp.where(
                hot_t, meta[j + 1 : j + 2, :], 0.0
            ).astype(BF16)
        chunks = half_img // (192 if count == 48 else 128)
        few, images = (half_src // chunks, half_img // chunks)
        for chunk in range(chunks):
            span = slice(chunk * images, (chunk + 1) * images)
            src = slice(side * half_src + chunk * few, side * half_src + (chunk + 1) * few)
            half_angle = jnp.dot(pick[span], normal_ref[...], preferred_element_type=F32)
            gain = cols[span, 4:5]
            bend = jnp.tanh(half_angle)
            refl = (jnp.log2(1.0 - bend) - 1.0) * (gain * (-LOG_2 / sharpness))
            sigma = bend * (gain * 0.5) + gain * 0.5
            seen = jnp.concatenate(
                [
                    pixels_ref[src, q * count : q * count + count, :].reshape(images, LANES)
                    for q in range(QUARTERS)
                ],
                axis=1,
            ).astype(F32)
            w_ref[span, :SLAB] = (seen * sigma).astype(BF16)
            w_ref[span, SLAB:] = (refl * sigma).astype(BF16)
            plain_ref[:, :SLAB] += jnp.sum((seen * refl).reshape(-1, 8, SLAB), axis=0)
            plain_ref[:, SLAB:] += jnp.sum((refl * refl).reshape(-1, 8, SLAB), axis=0)

    def back(w_ref, p_ref):
        sums_ref[...] += jnp.dot(p_ref[...], w_ref[...], preferred_element_type=F32)

    @pl.when(step == 0)
    def start():
        second_w[...] = jnp.zeros_like(second_w)
        second_p[...] = jnp.zeros_like(second_p)

    back(second_w, second_p)
    front(0, first_w, first_p)
    back(first_w, first_p)
    front(1, second_w, second_p)

    @pl.when(step == steps - 1)
    def finish():
        back(second_w, second_p)


def first_kernel(
    me_ref, meta_ref, pixels_ref, around_ref, lit_ref,
    sums_ref, plain_ref, normal_ref, slopes_ref, rows_ref, *work,
):
    @pl.when(pl.program_id(0) == 0)
    def start():
        sums_ref[...] = jnp.zeros_like(sums_ref)
        plain_ref[...] = jnp.zeros_like(plain_ref)
        slab_normals(me_ref[0], around_ref, lit_ref, normal_ref, slopes_ref, rows_ref)

    sum_images(
        0, pl.program_id(0), STEPS[0], meta_ref, pixels_ref, normal_ref, sums_ref, plain_ref, work
    )


def second_kernel(
    me_ref, meta_ref, pixels_ref, around_ref, lit_ref, sums_in, plain_in,
    reply_ref, sums_ref, plain_ref, normal_ref, slopes_ref, rows_ref, *work,
):
    @pl.when(pl.program_id(0) == 0)
    def start():
        sums_ref[...] = sums_in[...]
        plain_ref[...] = plain_in[...]
        slab_normals(me_ref[0], around_ref, lit_ref, normal_ref, slopes_ref, rows_ref)

    sum_images(
        1, pl.program_id(0), STEPS[1], meta_ref, pixels_ref, normal_ref, sums_ref, plain_ref, work
    )

    @pl.when(pl.program_id(0) == pl.num_programs(0) - 1)
    def finish():
        slab_reply(me_ref[0], lit_ref, slopes_ref, sums_ref, plain_ref, reply_ref)


SUMS = ((3 * DEVICES, 2 * SLAB), F32)
PLAIN = ((8, 2 * SLAB), F32)
NORMALS = ((6 * DEVICES, SLAB), BF16)
SLOPES = ((3, DEVICES, SLAB), F32)
ROWS = ((4, DEVICES, TILE), F32)


def kept(shape):
    return pl.BlockSpec(shape, lambda s: (0,) * len(shape))


def sum_call(part, kernel, inputs, specs, outs, scratch):
    count, sources = PARTS[part][1], SUM_SRC[part]
    half = sources * count // 2
    rows = QUARTERS * count + (EXTRA if part == 0 else 0)
    cells = DEVICES * count * SLAB
    return pl.pallas_call(
        kernel,
        grid=(DEVICES // sources,),
        in_specs=[
            pl.BlockSpec(memory_space=pltpu.SMEM),
            pl.BlockSpec((8, sources * count), lambda s: (0, s)),
            pl.BlockSpec((sources, rows, LANES), lambda s: (s, 0, 0)),
        ]
        + specs,
        out_specs=[kept(shape) for shape, dtype in outs],
        out_shape=[jax.ShapeDtypeStruct(shape, dtype) for shape, dtype in outs],
        scratch_shapes=[pltpu.VMEM(shape, dtype) for shape, dtype in scratch]
        + [pltpu.VMEM((half, 2 * SLAB), BF16)] * 2
        + [pltpu.VMEM((3 * DEVICES, half), BF16)] * 2,
        compiler_params=pltpu.CompilerParams(vmem_limit_bytes=26 * 1024 * 1024),
        cost_estimate=pl.CostEstimate(
            flops=2 * 12 * DEVICES * cells, bytes_accessed=4 * cells, transcendentals=2 * cells
        ),
    )(*inputs)


def first_sums(me, meta, pixels, around, lit):
    return sum_call(
        0,
        first_kernel,
        (me, meta, pixels, around, lit),
        [kept((DEVICES, 16, LANES)), kept((DEVICES, SLAB))],
        (SUMS, PLAIN),
        (NORMALS, SLOPES, ROWS),
    )


def second_sums(me, meta, pixels, around, lit, sums, plain):
    return sum_call(
        1,
        second_kernel,
        (me, meta, pixels, around, lit, sums, plain),
        [kept((DEVICES, 16, LANES)), kept((DEVICES, SLAB)), kept(SUMS[0]), kept(PLAIN[0])],
        (((DEVICES, REPLY, LANES), BF16),),
        (SUMS, PLAIN, NORMALS, SLOPES, ROWS),
    )[0]


def both_kernel(
    me_ref, meta_ref, pixels_ref, meta_rest, pixels_rest, around_ref, lit_ref,
    reply_ref, sums_ref, plain_ref, normal_ref, slopes_ref, rows_ref, *work,
):
    step = pl.program_id(0)

    @pl.when(step == 0)
    def start():
        sums_ref[...] = jnp.zeros_like(sums_ref)
        plain_ref[...] = jnp.zeros_like(plain_ref)
        slab_normals(me_ref[0], around_ref, lit_ref, normal_ref, slopes_ref, rows_ref)

    @pl.when(step < STEPS[0])
    def first():
        sum_images(
            0, step, STEPS[0], meta_ref, pixels_ref, normal_ref, sums_ref, plain_ref, work[:4]
        )

    @pl.when(step >= STEPS[0])
    def second():
        later = step - STEPS[0]
        sum_images(
            1, later, STEPS[1], meta_rest, pixels_rest, normal_ref, sums_ref, plain_ref, work[4:]
        )

    @pl.when(step == STEPS[0] + STEPS[1] - 1)
    def finish():
        slab_reply(me_ref[0], lit_ref, slopes_ref, sums_ref, plain_ref, reply_ref)


def both_sums(me, metas, pixels, around, lit):
    places = (
        lambda s: jnp.minimum(s, STEPS[0] - 1),
        lambda s: jnp.maximum(s - STEPS[0], 0),
    )
    specs, scratch = [pl.BlockSpec(memory_space=pltpu.SMEM)], []
    for part in range(2):
        count, sources, place = PARTS[part][1], SUM_SRC[part], places[part]
        rows = QUARTERS * count + (EXTRA if part == 0 else 0)
        specs.append(pl.BlockSpec((8, sources * count), lambda s, place=place: (0, place(s))))
        specs.append(
            pl.BlockSpec((sources, rows, LANES), lambda s, place=place: (place(s), 0, 0))
        )
        scratch += [pltpu.VMEM((sources * count // 2, 2 * SLAB), BF16)] * 2
        scratch += [pltpu.VMEM((3 * DEVICES, sources * count // 2), BF16)] * 2
    return pl.pallas_call(
        both_kernel,
        grid=(STEPS[0] + STEPS[1],),
        in_specs=specs + [kept((DEVICES, 16, LANES)), kept((DEVICES, SLAB))],
        out_specs=kept((DEVICES, REPLY, LANES)),
        out_shape=jax.ShapeDtypeStruct((DEVICES, REPLY, LANES), BF16),
        scratch_shapes=[
            pltpu.VMEM(shape, dtype) for shape, dtype in (SUMS, PLAIN, NORMALS, SLOPES, ROWS)
        ]
        + scratch,
        compiler_params=pltpu.CompilerParams(vmem_limit_bytes=26 * 1024 * 1024),
    )(me, metas[0], pixels[0], metas[1], pixels[1], around, lit)


def owner_kernel(final, *refs):
    got_ref, surface_ref, hits_ref, height_ref, ends_ref, sides_ref = refs[:6]
    outs, (model_ref, misfit_ref, scalar_ref, mixed_ref) = refs[6:-4], refs[-4:]
    swap, short_swap = swap_matrix(), swap_matrix(16, 8)
    for group in range(DEVICES // 16):
        span = slice(group * 16, group * 16 + 16)
        rows = []
        for matrix, start, count in ((swap, 0, 16), (short_swap, 16, 8)):
            block = got_ref[span, start : start + count, :].reshape(16 * count, LANES)
            turned = jnp.dot(matrix, block, preferred_element_type=F32)
            rows += [turned[j * 16 : j * 16 + 16] for j in range(count)]
        for j in range(10):
            model_ref[j, span] = rows[j]
            misfit_ref[j, span] = rows[10 + j]
        scalar_ref[span] = rows[20]
    scalars = scalar_ref[...]
    cross = scalars[:, 0:1] + scalars[:, 1:2] + scalars[:, 2:3]
    power = scalars[:, 3:4] + scalars[:, 4:5] + scalars[:, 5:6]
    albedo = jnp.sum(cross, keepdims=True) / jnp.sum(power, keepdims=True)
    rest = albedo * (albedo - own_albedo(cross, power))

    def grad(j):
        return jnp.concatenate(
            [albedo * misfit_ref[i] + rest * model_ref[i] for i in (j, j + 1)], axis=1
        )

    row = iota_of((DEVICES, TILE), 0)
    lane = iota_of((DEVICES, TILE), 1)
    along_even, along_odd, halo = grad(4), grad(6), grad(8)
    before = jnp.where(row == 0, pltpu.roll(halo, 1, 0), pltpu.roll(along_odd, 1, 0))
    after = jnp.where(
        row == DEVICES - 1,
        pltpu.roll(halo, DEVICES - 1, 0),
        pltpu.roll(along_even, DEVICES - 1, 0),
    )
    data = (grad(0) + (before - along_odd) * 0.5, grad(2) + (along_even - after) * 0.5)
    old = (surface_ref[:DEVICES], surface_ref[DEVICES:])
    above = jnp.where(row == 0, ends_ref[0:1], pltpu.roll(old[1], 1, 0))
    below = jnp.where(row == DEVICES - 1, ends_ref[1:2], pltpu.roll(old[0], DEVICES - 1, 0))
    vertical = (above + old[1], old[0] + below)
    new = []
    for part in range(2):
        span = slice(part * DEVICES, (part + 1) * DEVICES)
        left = jnp.where(lane == 0, sides_ref[span, 0:1], pltpu.roll(old[part], 1, 1))
        right = jnp.where(
            lane == TILE - 1, sides_ref[span, 1:2], pltpu.roll(old[part], TILE - 1, 1)
        )
        laplace = vertical[part] + left + right - 4.0 * old[part]
        laser = hits_ref[span] * old[part] - height_ref[span]
        new.append(
            old[part]
            - step_size * (data[part] - smooth_weight * laplace + laser_weight * laser)
        )
    if final:
        for part in range(2):
            for half in range(2):
                lanes = slice(half * LANES, half * LANES + LANES)
                mixed_ref[pl.ds(half * TILE + part, DEVICES, 2), :] = new[part][:, lanes]
        for half in range(2):
            outs[0][:, half * LANES : half * LANES + LANES] = mixed_ref[
                half * TILE : half * TILE + TILE
            ]
        return
    outs[0][:DEVICES], outs[0][DEVICES:] = new[0], new[1]
    pieces = around_pieces(new[0], new[1])
    for group in range(DEVICES // 16):
        span = slice(group * 16, group * 16 + 16)
        outs[1][span] = swapped(swap, [item[span] for item in pieces])


def owner_update(final, got, surface, hits, height_sum, rims):
    above, below, left, right = rims
    ends = jnp.concatenate([above, below], axis=0)
    sides = jnp.concatenate([left, right], axis=1)
    out_shape = [jax.ShapeDtypeStruct((TILE, TILE), F32)]
    if not final:
        out_shape.append(jax.ShapeDtypeStruct((DEVICES, 16, LANES), BF16))
    return pl.pallas_call(
        functools.partial(owner_kernel, final),
        out_shape=out_shape,
        scratch_shapes=[
            pltpu.VMEM((10, DEVICES, LANES), F32),
            pltpu.VMEM((10, DEVICES, LANES), F32),
            pltpu.VMEM((DEVICES, LANES), F32),
            pltpu.VMEM((2 * TILE, LANES), F32),
        ],
        compiler_params=pltpu.CompilerParams(vmem_limit_bytes=16 * 1024 * 1024),
    )(got, surface, hits, height_sum, ends, sides)


def shot_sums(slots):
    cell = lax.broadcasted_iota(jnp.int32, (1, TILE), 1).astype(F32)
    present = slots[:, 4:5]
    in_row = jnp.where(slots[:, 0:1] == cell, 1.0, 0.0)
    in_col = jnp.where(slots[:, 1:2] == cell, 1.0, 0.0).astype(BF16)
    left = jnp.concatenate([in_row * slots[:, j : j + 1] * present for j in (4, 2, 3)], axis=1)
    both = lax.dot_general(
        left.astype(BF16), in_col, (((0,), (0,)), ((), ())), preferred_element_type=F32
    )
    return both[:TILE], both[TILE : 2 * TILE] + both[2 * TILE :]


def body(heights, shadow, image_tiles, image_dest, sun_gain, shot_dest, shot_pixel, shot_height):
    me = (lax.axis_index("row") * N_COL + lax.axis_index("col")).astype(jnp.int32)[None]
    packed, surface = pack(
        image_tiles,
        heights,
        shadow,
        image_dest.T,
        sun_gain.T,
        shot_dest.T,
        shot_pixel[None, :],
        shot_height[None, :],
    )
    rims = edges(surface)
    pixels = (exchange(packed), exchange(pack_rest(image_tiles)))
    extra = pixels[0][:, QUARTERS * PARTS[0][1] :, :]
    metas = []
    for start, count in PARTS:
        lists = [
            extra[:, row, at + start : at + start + count]
            for row, at in ((20, 0), (21, 0), (21, IMG), (22, 0), (22, IMG))
        ]
        meta = jnp.stack(lists).astype(F32).reshape(5, DEVICES * count)
        metas.append(jnp.pad(meta, ((0, 3), (0, 0))))
    slab_lit = extra[:, 16:20, :].reshape(DEVICES, SLAB).astype(F32)
    around = extra[:, 0:16, :]
    slots = extra[:, 23, : SHOT_CAP * 5].reshape(DEVICES * SHOT_CAP, 5).astype(F32)
    hits, height_sum = shot_sums(slots)
    begun = first_sums(me, metas[0], pixels[0], around, slab_lit)
    got = exchange(second_sums(me, metas[1], pixels[1], around, slab_lit, *begun))
    surface, around = owner_update(False, got, surface, hits, height_sum, rims)
    around = exchange(around)
    rims = edges(surface)
    got = exchange(both_sums(me, metas, pixels, around, slab_lit))
    return owner_update(True, got, surface, hits, height_sum, rims)[0]


def solution(mesh):
    placed = (
        P("row", "col"),
        P("row", "col"),
        P(("row", "col"), None, None),
        P(("row", "col"), None),
        P(("row", "col"), None),
        P(("row", "col"), None),
        P(("row", "col")),
        P(("row", "col")),
    )
    return jax.shard_map(
        body, mesh=mesh, in_specs=placed, out_specs=P("row", "col"), check_vma=False
    )
```
